1024 devices in a mesh: row: 32 (over z_lo, x, core), col: 8 (over y), rep: 4 (over z_hi).
Axes of the slice: x: 8, y: 8, z: 8 (z_hi: 4, z_lo: 2; z = z_hi * 2 + z_lo), core: 2. Of those that a mesh axis runs over, the one named last changes fastest.
Arguments:
- tokens: bfloat16 [1024, 8192], P(('row', 'rep'), 'col'), may hold values from -6 to 6
- cotangent: bfloat16 [1024, 8192], P(('row', 'rep'), 'col'), may hold values from -0.59765625 to 0.59765625
- pad_mask: int32 [1024], P(('row', 'rep')), may hold values 0 or 1
- rewards: int32 [8, 8], replicated, may hold values from -4 to 4
- selected: int32 [8], replicated, may hold values from 0 to 7
- gate_weight: bfloat16 [8192, 16384], P('col', 'row'), may hold values from -0.0625 to 0.0625
- up_weight: bfloat16 [8192, 16384], P('col', 'row'), may hold values from -0.0625 to 0.0625
- down_weight: bfloat16 [16384, 8192], P('row', 'col'), may hold values from -0.046875 to 0.046875
Outputs:
- gate_grad: float32 [8192, 16384], P(('col', 'rep'), 'row')
- up_grad: float32 [8192, 16384], P(('col', 'rep'), 'row')
- down_grad: float32 [16384, 8192], P('row', ('col', 'rep'))
The draws below stay inside these ranges and needn't reach their ends.
All inputs are finite; a program needn't handle non-finite values. No bound on the sum of `pad_mask` on one device may be relied on, other than what follows from the above.
Results may differ from the reference program's by a relative error of at most 0.0035.
Values may be sent and summed in bfloat16 or wider, within the bound.
No kernel may reach another device: no remote copies, remote signals or barrier semaphores. Data moves between devices by JAX's collectives and lax.ppermute only.
A program may use at most 32 MiB of HBM per device.

```python
import jax
import jax.numpy as jnp

D = 8192
FF = 16384
SAMPLES = 8
COMP_LEN = 16
TOKENS = 1024
PROMPTS = 8


def plant(drawn, key, low, high):
    extent = drawn.shape
    spot = [jax.random.randint(jax.random.fold_in(key, axis), (), 0, extent[axis]) for axis in range(len(extent))]
    drawn = drawn.at[tuple(spot)].set(low)
    longest = extent.index(max(extent))
    spot[longest] = (spot[longest] + 1) % extent[longest]
    return drawn.at[tuple(spot)].set(high)


def levels(rng, shape, cuts, smallest, largest):
    factor_of = 1.0
    for dim, shards_of in cuts:
        heights = jax.random.uniform(jax.random.fold_in(jax.random.fold_in(rng, 6), dim), (shards_of,), jnp.float32, smallest / len(cuts), largest / len(cuts))
        factor_of = factor_of * jnp.repeat(jnp.exp(heights), shape[dim] // shards_of).reshape((-1,) + (1,) * (len(shape) - 1 - dim))
    return factor_of


def centred(own_key, shape, spread, bound, split=(), kind=jnp.bfloat16):
    factor_of = levels(own_key, shape, split, -0.22, 0.18) if split else 1.0
    values = jax.random.normal(own_key, shape, jnp.float32) * spread * factor_of
    return jnp.minimum(jnp.maximum(values, -bound), bound).astype(kind)


def setup_inputs(seed: int = 0) -> dict:
    streams_of = jax.random.split(jax.random.key(seed), 9)
    tokens = centred(streams_of[0], (TOKENS, D), 1.0, 6.0, ((0, 128), (1, 8)))
    cotangent = centred(streams_of[1], (TOKENS, D), 0.1, 0.59765625, ((0, 128), (1, 8)))
    pad_mask = plant((jax.random.randint(streams_of[2], (TOKENS,), 0, 4) < 3).astype(jnp.int32), jax.random.fold_in(streams_of[2], 1), 0, 1)
    rewards = plant(jax.random.randint(streams_of[3], (PROMPTS, SAMPLES), -4, 5), jax.random.fold_in(streams_of[3], 1), -4, 4).astype(jnp.int32)
    selected = plant(jax.random.randint(streams_of[4], (PROMPTS,), 0, SAMPLES), jax.random.fold_in(streams_of[4], 1), 0, SAMPLES - 1).astype(jnp.int32)
    gate_weight = centred(streams_of[5], (D, FF), D ** -0.5, 0.0625, ((0, 8), (1, 32)))
    up_weight = centred(streams_of[6], (D, FF), D ** -0.5, 0.0625, ((0, 8), (1, 32)))
    down_weight = centred(streams_of[7], (FF, D), FF ** -0.5, 0.046875, ((0, 32), (1, 8)))
    return dict(tokens=tokens, cotangent=cotangent, pad_mask=pad_mask, rewards=rewards, selected=selected, gate_weight=gate_weight, up_weight=up_weight, down_weight=down_weight)


def token_weights(pad_mask, rewards, selected):
    position = jnp.arange(TOKENS, dtype=jnp.int32)
    completion = position // COMP_LEN
    prompt_index = completion // SAMPLES
    sample_index = completion % SAMPLES
    reward_value = rewards.reshape(-1)[completion].astype(jnp.float32)
    chosen_flag = (selected[prompt_index] == sample_index).astype(jnp.float32)
    return pad_mask.astype(jnp.float32) * (reward_value / 4.0 + chosen_flag)


def reference(tokens, cotangent, pad_mask, rewards, selected, gate_weight, up_weight, down_weight):
    weight = token_weights(pad_mask, rewards, selected)
    grads = (weight[:, None] * cotangent.astype(jnp.float32)).astype(jnp.bfloat16)
    gate_value = jnp.dot(tokens, gate_weight, preferred_element_type=jnp.float32)
    up_value = jnp.dot(tokens, up_weight, preferred_element_type=jnp.float32)
    back_value = jnp.dot(grads, down_weight.T, preferred_element_type=jnp.float32)
    sigmoid_gate = jax.nn.sigmoid(gate_value)
    active = gate_value * sigmoid_gate
    hidden = (active * up_value).astype(jnp.bfloat16)
    gate_back = (back_value * up_value * sigmoid_gate * (1.0 + gate_value * (1.0 - sigmoid_gate))).astype(jnp.bfloat16)
    up_back = (back_value * active).astype(jnp.bfloat16)
    gate_grad = jnp.dot(tokens.T, gate_back, preferred_element_type=jnp.float32)
    up_grad = jnp.dot(tokens.T, up_back, preferred_element_type=jnp.float32)
    down_grad = jnp.dot(hidden.T, grads, preferred_element_type=jnp.float32)
    return (gate_grad, up_grad, down_grad)
```

```python
import jax
import jax.numpy as jnp
from jax import lax
from jax.experimental import pallas as pl
from jax.experimental.pallas import tpu as pltpu
from jax.sharding import Mesh
from jax.sharding import PartitionSpec as P

SAMPLES = 8
COMP_LEN = 16
CORES = 2
Z_LO = 2
SCALE_UP = 128.0
SCALE_BACK = 1024.0
ROW = ("zlo", "x", "core")
bf16 = jnp.bfloat16
f32 = jnp.float32


def shift(value, axis, step):
    n = lax.axis_size(axis)
    return lax.ppermute(value, axis, [(i, (i + step) % n) for i in range(n)])


def prepare_kernel(block_ref, rewards_ref, selected_ref, pad_ref, tokens_ref, cotangent_ref, out_ref):
    rows, width = tokens_ref.shape
    completion = block_ref[0] * rows // COMP_LEN
    prompt = completion // SAMPLES
    sample = completion % SAMPLES
    reward = rewards_ref[prompt, sample].astype(f32)
    chosen = jnp.where(selected_ref[prompt] == sample, 1.0, 0.0)
    factor = reward / 4.0 + chosen
    weight = pad_ref[...].astype(f32) * factor
    grads = (weight * cotangent_ref[...].astype(f32)).astype(bf16)
    for copy in range(out_ref.shape[0]):
        out_ref[copy, :, :width] = tokens_ref[...]
        out_ref[copy, :, width:] = grads


def prepare(copies, block, rewards, selected, pad_mask, tokens, cotangent):
    rows, width = tokens.shape
    smem = pl.BlockSpec(memory_space=pltpu.SMEM)
    vmem = pl.BlockSpec(memory_space=pltpu.VMEM)
    return pl.pallas_call(
        prepare_kernel,
        out_shape=jax.ShapeDtypeStruct((copies, rows, 2 * width), bf16),
        in_specs=[smem, smem, smem, vmem, vmem, vmem],
        out_specs=vmem,
    )(block.reshape(1), rewards, selected, pad_mask.reshape(rows, 1), tokens, cotangent)


def unit_values(summed, unit_width):
    gate_value = summed[:, :unit_width] * (1.0 / SCALE_UP)
    up_value = summed[:, unit_width : 2 * unit_width] * (1.0 / SCALE_UP)
    back_value = summed[:, 2 * unit_width :] * (1.0 / SCALE_BACK)
    sigmoid_gate = jax.nn.sigmoid(gate_value)
    active = gate_value * sigmoid_gate
    hidden = (active * up_value).astype(bf16)
    gate_back = (
        back_value * up_value * sigmoid_gate * (1.0 + gate_value * (1.0 - sigmoid_gate))
    ).astype(bf16)
    up_back = (back_value * active).astype(bf16)
    return jnp.concatenate([hidden, gate_back, up_back], axis=1)


def body(tokens, cotangent, pad_mask, rewards, selected, gate_weight, up_weight, down_weight):
    n_y = lax.axis_size("y")
    n_k = lax.axis_size("zhi")
    y = lax.axis_index("y")
    k = lax.axis_index("zhi")
    rows, width = tokens.shape
    units = gate_weight.shape[1]
    block = lax.axis_index(ROW) * n_k + k
    copies = lax.axis_size(("zlo", "x"))
    spread = prepare(copies, block, rewards, selected, pad_mask, tokens, cotangent)
    mine = lax.all_to_all(spread, ("zlo", "x"), 0, 0)
    other = shift(mine, "core", 1)
    half = copies * rows
    part = half // n_y

    pieces = []
    halves = [mine.reshape(half, 2 * width), other.reshape(half, 2 * width)]
    for rows_in in halves:
        gate = jnp.dot(rows_in[:, :width], gate_weight, preferred_element_type=f32) * SCALE_UP
        up = jnp.dot(rows_in[:, :width], up_weight, preferred_element_type=f32) * SCALE_UP
        back = SCALE_BACK * lax.dot_general(
            rows_in[:, width:], down_weight, (((1,), (1,)), ((), ())), preferred_element_type=f32
        )
        whole = jnp.concatenate([gate, up, back], axis=1).astype(jnp.float16)
        pieces.append(whole.reshape(n_y, part, 3 * units))
    sums = lax.all_to_all(jnp.concatenate(pieces, axis=1), "y", 0, 0)
    values = unit_values(jnp.sum(sums.astype(f32), axis=0), units)
    share = 2 * part

    replicas = lax.all_to_all(
        jnp.broadcast_to(values[None], (n_k, share, 3 * units)), "zhi", 0, 0
    )

    chunks = []
    for c in range(2):
        held = replicas[c * n_k // 2 : (c + 1) * n_k // 2]
        right = left = held
        at = {0: held}
        for s in range(1, n_y // 2):
            right = shift(right, "y", 1)
            left = shift(left, "y", -1)
            at[n_y - s] = right
            at[s] = left
        top = shift(right[:1], "y", 1)
        low = shift(left[1:], "y", -1)
        at[n_y // 2] = jnp.concatenate([top, low], axis=0)
        chunks.append(jnp.stack([at[r] for r in range(n_y)], axis=0))
    every = jnp.concatenate(chunks, axis=1).reshape(n_y * n_k * share, 3 * units)

    quarter = width // n_k
    both = jnp.stack([h.reshape(n_y, part, 2, n_k, quarter) for h in halves], axis=1)
    got = []
    for t in range(n_k):
        owner = (k - t) % n_k
        cut = lax.dynamic_index_in_dim(both, owner, axis=4, keepdims=False)
        cut = cut.reshape(n_y, share, 2 * quarter)
        got.append(cut if t == 0 else shift(cut, "zhi", -t))
    near = jnp.stack(got + got[:-1], axis=1)
    near = lax.dynamic_slice_in_dim(near, (n_k - k) % n_k, n_k, axis=1)
    near = jnp.concatenate([near, near[:-1]], axis=0)
    near = lax.dynamic_slice_in_dim(near, y, n_y, axis=0)
    near = near.reshape(n_y * n_k * share, 2 * quarter)

    contract = (((0,), (0,)), ((), ()))
    gate_grad = lax.dot_general(
        near[:, :quarter], every[:, units : 2 * units], contract, preferred_element_type=f32
    )
    up_grad = lax.dot_general(
        near[:, :quarter], every[:, 2 * units :], contract, preferred_element_type=f32
    )
    down_grad = lax.dot_general(
        every[:, :units], near[:, quarter:], contract, preferred_element_type=f32
    )
    return (gate_grad, up_grad, down_grad)


def solution(mesh):
    n_row, n_col, n_rep = mesh.devices.shape
    fine = Mesh(
        mesh.devices.reshape(Z_LO, n_row // (Z_LO * CORES), CORES, n_col, n_rep),
        ("zlo", "x", "core", "y", "zhi"),
    )
    blocks = ROW + ("zhi",)
    placed = (
        P(blocks, "y"),
        P(blocks, "y"),
        P(blocks),
        P(),
        P(),
        P("y", ROW),
        P("y", ROW),
        P(ROW, "y"),
    )
    return jax.shard_map(
        body,
        mesh=fine,
        in_specs=placed,
        out_specs=(P(("y", "zhi"), ROW), P(("y", "zhi"), ROW), P(ROW, ("y", "zhi"))),
        check_vma=False,
    )
```

```python
import functools

import jax
import jax.numpy as jnp
from jax import lax
from jax.experimental import pallas as pl
from jax.experimental.pallas import tpu as pltpu
from jax.sharding import Mesh
from jax.sharding import PartitionSpec as P

SAMPLES = 8
COMP_LEN = 16
CORES = 2
Z_LO = 2
SCALE_UP = 128.0
SCALE_BACK = 1024.0
ROW = ("zlo", "x", "core")
bf16 = jnp.bfloat16
f16 = jnp.float16
f32 = jnp.float32


def shift(value, axis, step):
    n = lax.axis_size(axis)
    return lax.ppermute(value, axis, [(i, (i + step) % n) for i in range(n)])


def prepare_kernel(block_ref, rewards_ref, selected_ref, pad_ref, tokens_ref, cotangent_ref, x_ref, g_ref):
    rows = tokens_ref.shape[0]
    completion = block_ref[0] * rows // COMP_LEN
    prompt = completion // SAMPLES
    sample = completion % SAMPLES
    reward = rewards_ref[prompt, sample].astype(f32)
    chosen = jnp.where(selected_ref[prompt] == sample, 1.0, 0.0)
    factor = reward / 4.0 + chosen
    row = lax.broadcasted_iota(jnp.int32, (rows, 1), 0)
    weight = jnp.zeros((rows, 1), f32)
    for n in range(rows):
        weight = jnp.where(row == n, pad_ref[n].astype(f32) * factor, weight)
    grads = (weight * cotangent_ref[...].astype(f32)).astype(bf16)
    for copy in range(x_ref.shape[0]):
        x_ref[copy] = tokens_ref[...]
        g_ref[copy] = grads


def prepare(copies, block, rewards, selected, pad_mask, tokens, cotangent):
    smem = pl.BlockSpec(memory_space=pltpu.SMEM)
    vmem = pl.BlockSpec(memory_space=pltpu.VMEM)
    out = jax.ShapeDtypeStruct((copies,) + tokens.shape, bf16)
    return pl.pallas_call(
        prepare_kernel,
        out_shape=(out, out),
        in_specs=[smem, smem, smem, smem, vmem, vmem],
        out_specs=(vmem, vmem),
    )(block.reshape(1), rewards, selected, pad_mask, tokens, cotangent)


def quarters_kernel(order, place_ref, x0_ref, x1_ref, g0_ref, g1_ref, *out_refs):
    n_k = len(out_refs)
    n_y = len(order)
    part = x0_ref.shape[0] // n_y
    quarter = x0_ref.shape[1] // n_k
    y = place_ref[0]
    k = place_ref[1]
    for t in range(n_k):
        owner = lax.rem(k + (n_k - t), n_k)
        lanes = pl.ds(pl.multiple_of(owner * quarter, quarter), quarter)
        for spot, r in enumerate(order):
            share = lax.rem(y + r, n_y)
            rows = pl.ds(pl.multiple_of(share * part, part), part)
            for c, (x_ref, g_ref) in enumerate(((x0_ref, g0_ref), (x1_ref, g1_ref))):
                to = slice((2 * spot + c) * part, (2 * spot + c + 1) * part)
                out_refs[t][to, :quarter] = x_ref[rows, lanes]
                out_refs[t][to, quarter:] = g_ref[rows, lanes]


def cut_quarters(order, n_k, place, x0, x1, g0, g1):
    rows, width = x0.shape
    vmem = pl.BlockSpec(memory_space=pltpu.VMEM)
    out = jax.ShapeDtypeStruct((2 * rows, 2 * width // n_k), bf16)
    return pl.pallas_call(
        functools.partial(quarters_kernel, order),
        out_shape=(out,) * n_k,
        in_specs=[pl.BlockSpec(memory_space=pltpu.SMEM)] + [vmem] * 4,
        out_specs=(vmem,) * n_k,
    )(place, x0, x1, g0, g1)


def unit_values(gate_value, up_value, back_value):
    sigmoid_gate = jax.nn.sigmoid(gate_value)
    active = gate_value * sigmoid_gate
    hidden = (active * up_value).astype(bf16)
    gate_back = (
        back_value * up_value * sigmoid_gate * (1.0 + gate_value * (1.0 - sigmoid_gate))
    ).astype(bf16)
    up_back = (back_value * active).astype(bf16)
    return jnp.concatenate([hidden, gate_back, up_back], axis=1)


def after(value, *others):
    return lax.optimization_barrier((value,) + others)[0]


def body(tokens, cotangent, pad_mask, rewards, selected, gate_weight, up_weight, down_weight):
    n_y = lax.axis_size("y")
    n_k = lax.axis_size("zhi")
    y = lax.axis_index("y")
    k = lax.axis_index("zhi")
    rows, width = tokens.shape
    units = gate_weight.shape[1]
    block = lax.axis_index(ROW) * n_k + k
    copies = lax.axis_size(("zlo", "x"))
    half = copies * rows
    part = half // n_y
    share = 2 * part
    quarter = width // n_k

    x_spread, g_spread = prepare(copies, block, rewards, selected, pad_mask, tokens, cotangent)
    x0 = lax.all_to_all(x_spread, ("zlo", "x"), 0, 0)
    g0 = lax.all_to_all(g_spread, ("zlo", "x"), 0, 0)
    x1 = shift(x0, "core", 1).reshape(half, width)
    g1 = shift(g0, "core", 1).reshape(half, width)
    x0 = x0.reshape(half, width)
    g0 = g0.reshape(half, width)

    forward = []
    backward = []
    for x in (x0, x1):
        gate = jnp.dot(x, gate_weight, preferred_element_type=f32) * SCALE_UP
        up = jnp.dot(x, up_weight, preferred_element_type=f32) * SCALE_UP
        both = jnp.concatenate([gate.astype(f16), up.astype(f16)], axis=1)
        forward.append(both.reshape(n_y, part, 2 * units))
    for g in (g0, g1):
        back = lax.dot_general(g, down_weight, (((1,), (1,)), ((), ())), preferred_element_type=f32)
        backward.append((back * SCALE_BACK).astype(f16).reshape(n_y, part, units))
    sums = lax.all_to_all(jnp.concatenate(forward, axis=1), "y", 0, 0)
    back_sums = lax.all_to_all(jnp.concatenate(backward, axis=1), "y", 0, 0)
    sums = jnp.sum(sums.astype(f32), axis=0) * (1.0 / SCALE_UP)
    back_sums = jnp.sum(back_sums.astype(f32), axis=0) * (1.0 / SCALE_BACK)
    values = unit_values(sums[:, :units], sums[:, units:], back_sums)

    replicas = lax.all_to_all(
        jnp.broadcast_to(values[None], (n_k, share, 3 * units)), "zhi", 0, 0
    )
    a_right = shift(values, "y", 1)
    a_left = shift(values, "y", -1)
    own = {0: values, n_y - 1: a_right, 1: a_left}

    turned = jnp.concatenate([replicas, replicas[:-1]], axis=0)
    near = lax.dynamic_slice_in_dim(turned, k + 1, n_k - 1, axis=0)
    near = near.reshape((n_k - 1) * share, 3 * units)
    rest = near.shape[0]
    far = {0: near}

    order = [0]
    for s in range(1, n_y // 2):
        order += [s, n_y - s]
    order.append(n_y // 2)
    pieces = cut_quarters(order, n_k, jnp.stack([y, k]), x0, x1, g0, after(g1, values))

    right = jnp.concatenate([near, a_right], axis=0)
    left = jnp.concatenate([near, a_left[part:], a_left[:part]], axis=0)
    got = [pieces[0]]
    for s in range(1, n_y // 2):
        if s == n_y // 2 - 1:
            right = right[: rest + part]
            left = left[: rest + part]
        right = shift(right, "y", 1)
        left = shift(left, "y", -1)
        far[n_y - s] = right[:rest]
        far[s] = left[:rest]
        if s == n_y // 2 - 1:
            own[n_y // 2] = jnp.concatenate([right[rest:], left[rest:]], axis=0)
        else:
            own[n_y - s - 1] = right[rest:]
            own[s + 1] = jnp.concatenate([left[rest + part :], left[rest : rest + part]], axis=0)
        if s < n_k:
            got.append(shift(after(pieces[s], right, left), "zhi", -s))
    top = shift(right[: rest // 2], "y", 1)
    low = shift(left[rest // 2 : rest], "y", -1)

    main = jnp.concatenate([v for r in order[:-1] for v in (own[r], far[r])], axis=0)
    last = jnp.concatenate([own[n_y // 2], top, low], axis=0)
    inputs = jnp.stack([v.reshape(n_y, share, 2 * quarter) for v in got], axis=1)
    inputs = inputs.reshape(n_y * n_k * share, 2 * quarter)
    cut = main.shape[0]
    contract = (((0,), (0,)), ((), ()))

    def product(a, b):
        return lax.dot_general(a, b, contract, preferred_element_type=f32)

    early = inputs[:cut]
    late = inputs[cut:]
    gate_grad = product(early[:, :quarter], main[:, units : 2 * units])
    up_grad = product(early[:, :quarter], main[:, 2 * units :])
    down_grad = product(main[:, :units], early[:, quarter:])
    gate_grad += product(late[:, :quarter], last[:, units : 2 * units])
    up_grad += product(late[:, :quarter], last[:, 2 * units :])
    down_grad += product(last[:, :units], late[:, quarter:])
    return (gate_grad, up_grad, down_grad)


def solution(mesh):
    n_row, n_col, n_rep = mesh.devices.shape
    fine = Mesh(
        mesh.devices.reshape(Z_LO, n_row // (Z_LO * CORES), CORES, n_col, n_rep),
        ("zlo", "x", "core", "y", "zhi"),
    )
    blocks = ROW + ("zhi",)
    placed = (
        P(blocks, "y"),
        P(blocks, "y"),
        P(blocks),
        P(),
        P(),
        P("y", ROW),
        P("y", ROW),
        P(ROW, "y"),
    )
    return jax.shard_map(
        body,
        mesh=fine,
        in_specs=placed,
        out_specs=(P(("y", "zhi"), ROW), P(("y", "zhi"), ROW), P(ROW, ("y", "zhi"))),
        check_vma=False,
    )
```

```python
import functools

import jax
import jax.numpy as jnp
from jax import lax
from jax.experimental import pallas as pl
from jax.experimental.pallas import tpu as pltpu
from jax.sharding import Mesh
from jax.sharding import PartitionSpec as P

SAMPLES = 8
COMP_LEN = 16
CORES = 2
Z_LO = 2
SCALE_UP = 128.0
SCALE_BACK = 1024.0
ROW = ("zlo", "x", "core")
bf16 = jnp.bfloat16
f16 = jnp.float16
f32 = jnp.float32


def shift(value, axis, step):
    n = lax.axis_size(axis)
    return lax.ppermute(value, axis, [(i, (i + step) % n) for i in range(n)])


def prepare_kernel(block_ref, rewards_ref, selected_ref, pad_ref, tokens_ref, cotangent_ref, all_ref, cut_ref):
    rows, width = tokens_ref.shape
    quarter = cut_ref.shape[2] // 2
    n_k = width // quarter
    completion = block_ref[0] * rows // COMP_LEN
    prompt = completion // SAMPLES
    sample = completion % SAMPLES
    reward = rewards_ref[prompt, sample].astype(f32)
    chosen = jnp.where(selected_ref[prompt] == sample, 1.0, 0.0)
    factor = reward / 4.0 + chosen
    row = lax.broadcasted_iota(jnp.int32, (rows, 1), 0)
    weight = jnp.zeros((rows, 1), f32)
    for n in range(rows):
        weight = jnp.where(row == n, pad_ref[n].astype(f32) * factor, weight)
    grads = (weight * cotangent_ref[...].astype(f32)).astype(bf16)
    for copy in range(all_ref.shape[0]):
        all_ref[copy, :, :width] = tokens_ref[...]
        all_ref[copy, :, width:] = grads
    for t in range(n_k):
        lanes = slice(t * quarter, (t + 1) * quarter)
        cut_ref[t, :, :quarter] = tokens_ref[:, lanes]
        cut_ref[t, :, quarter:] = grads[:, lanes]


def prepare(copies, n_k, block, rewards, selected, pad_mask, tokens, cotangent):
    rows, width = tokens.shape
    smem = pl.BlockSpec(memory_space=pltpu.SMEM)
    vmem = pl.BlockSpec(memory_space=pltpu.VMEM)
    return pl.pallas_call(
        prepare_kernel,
        out_shape=(
            jax.ShapeDtypeStruct((copies, rows, 2 * width), bf16),
            jax.ShapeDtypeStruct((n_k, rows, 2 * width // n_k), bf16),
        ),
        in_specs=[smem, smem, smem, smem, vmem, vmem],
        out_specs=(vmem, vmem),
    )(block.reshape(1), rewards, selected, pad_mask, tokens, cotangent)


def order_kernel(order, n_k, place_ref, pieces_ref, turned_ref):
    n_y = len(order)
    per = pieces_ref.shape[0] // (n_y * n_k * CORES)
    y = place_ref[0]
    k = place_ref[1]
    core = place_ref[2]

    def source(share, e, c, t):
        row = (share * per + e) * CORES + lax.rem(core + c, CORES)
        return row * n_k + lax.rem(t + n_k - k, n_k)

    spots = [(c, e) for c in range(CORES) for e in range(per)]
    at = 0
    for r in order:
        share = lax.rem(y + r, n_y)
        for t in range(n_k):
            for c, e in spots:
                turned_ref[at] = pieces_ref[source(share, e, c, t)]
                at += 1


def put_in_order(order, n_k, place, pieces):
    blocks, rows, both = pieces.shape
    vmem = pl.BlockSpec(memory_space=pltpu.VMEM)
    turned = pl.pallas_call(
        functools.partial(order_kernel, order, n_k),
        out_shape=jax.ShapeDtypeStruct((blocks, rows, both), bf16),
        in_specs=[pl.BlockSpec(memory_space=pltpu.SMEM), vmem],
        out_specs=vmem,
    )(place, pieces)
    return turned.reshape(blocks * rows, both)


def after(value, *others):
    return lax.optimization_barrier((value,) + others)[0]


def copies_to(value, axis):
    spread = jnp.broadcast_to(value[None], (lax.axis_size(axis),) + value.shape)
    return lax.all_to_all(spread, axis, 0, 0)


def body(tokens, cotangent, pad_mask, rewards, selected, gate_weight, up_weight, down_weight):
    n_y = lax.axis_size("y")
    n_k = lax.axis_size("zhi")
    y = lax.axis_index("y")
    rows, width = tokens.shape
    units = gate_weight.shape[1]
    k = lax.axis_index("zhi")
    block = lax.axis_index(ROW) * n_k + k
    copies = lax.axis_size(("zlo", "x"))
    half = copies * rows
    part = half // n_y
    share = 2 * part
    quarter = width // n_k

    spread, cut_spread = prepare(copies, n_k, block, rewards, selected, pad_mask, tokens, cotangent)
    mine = lax.all_to_all(spread, ("zlo", "x"), 0, 0)
    cuts = []
    for t in range(n_k):
        piece = lax.dynamic_index_in_dim(cut_spread, (k + n_k - t) % n_k, axis=0, keepdims=False)
        cuts.append(piece if t == 0 else shift(piece, "zhi", -t))
    cuts = jnp.stack(cuts, axis=0)
    mine, cuts = lax.optimization_barrier((mine, cuts))
    cuts = lax.all_gather(cuts, ROW, axis=0, tiled=True)
    other = shift(mine, "core", 1)

    pieces = []
    for rows_in in (mine.reshape(half, 2 * width), other.reshape(half, 2 * width)):
        gate = jnp.dot(rows_in[:, :width], gate_weight, preferred_element_type=f32) * SCALE_UP
        up = jnp.dot(rows_in[:, :width], up_weight, preferred_element_type=f32) * SCALE_UP
        back = SCALE_BACK * lax.dot_general(
            rows_in[:, width:], down_weight, (((1,), (1,)), ((), ())), preferred_element_type=f32
        )
        whole = jnp.concatenate([gate, up, back], axis=1).astype(f16)
        pieces.append(whole.reshape(n_y, part, 3 * units))
    partial_sums = jnp.concatenate(pieces, axis=1)
    sums = lax.all_to_all(partial_sums, "y", 0, 0)

    sums = jnp.sum(sums.astype(f32), axis=0)
    gate_value = sums[:, :units] * (1.0 / SCALE_UP)
    up_value = sums[:, units : 2 * units] * (1.0 / SCALE_UP)
    back_value = sums[:, 2 * units :] * (1.0 / SCALE_BACK)
    sigmoid_gate = jax.nn.sigmoid(gate_value)
    active = gate_value * sigmoid_gate
    hidden = (active * up_value).astype(bf16)
    gate_back = (
        back_value * up_value * sigmoid_gate * (1.0 + gate_value * (1.0 - sigmoid_gate))
    ).astype(bf16)
    up_back = (back_value * active).astype(bf16)

    values = jnp.concatenate([hidden, gate_back, up_back], axis=1)
    near = copies_to(values, "zhi").reshape(n_k * share, 3 * units)

    order = [0]
    for s in range(1, n_y // 2):
        order += [s, n_y - s]
    order.append(n_y // 2)
    place = jnp.stack([y, k, lax.axis_index("core")])

    right = left = near
    held = {0: near}
    for s in range(1, n_y // 2):
        right = shift(right, "y", 1)
        left = shift(left, "y", -1)
        held[n_y - s] = right
        held[s] = left
    middle = near.shape[0] // 2
    top = shift(right[:middle], "y", 1)
    low = shift(left[middle:], "y", -1)

    turned = put_in_order(order, n_k, place, after(cuts, top))

    contract = (((0,), (0,)), ((), ()))

    def product(a, b):
        return lax.dot_general(a, b, contract, preferred_element_type=f32)

    held[n_y // 2] = jnp.concatenate([top, low], axis=0)
    every = jnp.concatenate([held[r] for r in order], axis=0)
    gate_grad = product(turned[:, :quarter], every[:, units : 2 * units])
    up_grad = product(turned[:, :quarter], every[:, 2 * units :])
    down_grad = product(every[:, :units], turned[:, quarter:])
    return (gate_grad, up_grad, down_grad)


def solution(mesh):
    n_row, n_col, n_rep = mesh.devices.shape
    fine = Mesh(
        mesh.devices.reshape(Z_LO, n_row // (Z_LO * CORES), CORES, n_col, n_rep),
        ("zlo", "x", "core", "y", "zhi"),
    )
    blocks = ROW + ("zhi",)
    placed = (
        P(blocks, "y"),
        P(blocks, "y"),
        P(blocks),
        P(),
        P(),
        P("y", ROW),
        P("y", ROW),
        P(ROW, "y"),
    )
    return jax.shard_map(
        body,
        mesh=fine,
        in_specs=placed,
        out_specs=(P(("y", "zhi"), ROW), P(("y", "zhi"), ROW), P(ROW, ("y", "zhi"))),
        check_vma=False,
    )
```

```python
import functools

import jax
import jax.numpy as jnp
from jax import lax
from jax.experimental import pallas as pl
from jax.experimental.pallas import tpu as pltpu
from jax.sharding import Mesh
from jax.sharding import PartitionSpec as P

SAMPLES = 8
COMP_LEN = 16
CORES = 2
Z_LO = 2
SCALE_UP = 128.0
SCALE_BACK = 1024.0
ROW = ("zlo", "x", "core")
bf16 = jnp.bfloat16
f16 = jnp.float16
f32 = jnp.float32


def shift(value, axis, step):
    n = lax.axis_size(axis)
    return lax.ppermute(value, axis, [(i, (i + step) % n) for i in range(n)])


def prepare_kernel(block_ref, rewards_ref, selected_ref, pad_ref, tokens_ref, cotangent_ref, all_ref):
    rows, width = tokens_ref.shape
    completion = block_ref[0] * rows // COMP_LEN
    prompt = completion // SAMPLES
    sample = completion % SAMPLES
    reward = rewards_ref[prompt, sample].astype(f32)
    chosen = jnp.where(selected_ref[prompt] == sample, 1.0, 0.0)
    factor = reward / 4.0 + chosen
    row = lax.broadcasted_iota(jnp.int32, (rows, 1), 0)
    weight = jnp.zeros((rows, 1), f32)
    for n in range(rows):
        weight = jnp.where(row == n, pad_ref[n].astype(f32) * factor, weight)
    grads = (weight * cotangent_ref[...].astype(f32)).astype(bf16)
    for copy in range(all_ref.shape[0]):
        all_ref[copy, :, :width] = tokens_ref[...]
        all_ref[copy, :, width:] = grads


def in_vmem():
    return pl.BlockSpec(memory_space=pltpu.VMEM)


def in_smem():
    return pl.BlockSpec(memory_space=pltpu.SMEM)


def prepare(copies, block, rewards, selected, pad_mask, tokens, cotangent):
    rows, width = tokens.shape
    return pl.pallas_call(
        prepare_kernel,
        out_shape=jax.ShapeDtypeStruct((copies, rows, 2 * width), bf16),
        in_specs=[in_smem()] * 4 + [in_vmem()] * 2,
        out_specs=in_vmem(),
    )(block.reshape(1), rewards, selected, pad_mask, tokens, cotangent)


def cut_kernel(rows_ref, out_ref):
    n_k = out_ref.shape[0]
    width = rows_ref.shape[1] // 2
    quarter = width // n_k
    for t in range(n_k):
        out_ref[t, :, :quarter] = rows_ref[:, t * quarter : (t + 1) * quarter]
        out_ref[t, :, quarter:] = rows_ref[:, width + t * quarter : width + (t + 1) * quarter]


def cut_quarters(n_k, rows):
    return pl.pallas_call(
        cut_kernel,
        out_shape=jax.ShapeDtypeStruct((n_k, rows.shape[0], rows.shape[1] // n_k), bf16),
        in_specs=[in_vmem()],
        out_specs=in_vmem(),
    )(rows)


def order_kernel(order, place_ref, own_ref, other_ref, out_ref):
    n_k, rows, _ = own_ref.shape
    n_y = len(order)
    part = rows // n_y
    y = place_ref[0]
    at = 0
    for r in order:
        share = lax.rem(y + r, n_y)
        spot = pl.ds(pl.multiple_of(share * part, part), part)
        for t in range(n_k):
            for ref in (own_ref, other_ref):
                out_ref[at : at + part, :] = ref[t, spot, :]
                at += part


def put_in_order(order, y, own, other):
    n_k, rows, both = own.shape
    return pl.pallas_call(
        functools.partial(order_kernel, order),
        out_shape=jax.ShapeDtypeStruct((2 * n_k * rows, both), bf16),
        in_specs=[in_smem(), in_vmem(), in_vmem()],
        out_specs=in_vmem(),
    )(y.reshape(1), own, other)


def product(a, b):
    return lax.dot_general(a, b, (((0,), (0,)), ((), ())), preferred_element_type=f32)


def products_kernel(n, inputs_ref, *refs):
    value_refs = refs[:n]
    gate_ref, up_ref, down_ref, every_ref = refs[n:]
    at = 0
    for ref in value_refs:
        rows = ref.shape[0]
        every_ref[at : at + rows, :] = ref[...]
        at += rows
    units = gate_ref.shape[1]
    quarter = gate_ref.shape[0]
    tokens = inputs_ref[:, :quarter]
    down_ref[...] = product(every_ref[:, :units], inputs_ref[:, quarter:])
    gate_ref[...] = product(tokens, every_ref[:, units : 2 * units])
    up_ref[...] = product(tokens, every_ref[:, 2 * units :])


def products(inputs, values):
    rows, both = inputs.shape
    quarter = both // 2
    width = values[0].shape[1]
    units = width // 3
    wide = jax.ShapeDtypeStruct((quarter, units), f32)
    return pl.pallas_call(
        functools.partial(products_kernel, len(values)),
        out_shape=(wide, wide, jax.ShapeDtypeStruct((units, quarter), f32)),
        in_specs=[in_vmem()] * (1 + len(values)),
        out_specs=(in_vmem(),) * 3,
        scratch_shapes=[pltpu.VMEM((rows, width), bf16)],
        compiler_params=pltpu.CompilerParams(vmem_limit_bytes=40 * 1024 * 1024),
    )(inputs, *values)


def after(value, *others):
    return lax.optimization_barrier((value,) + others)[0]


def copies_to(value, axis):
    spread = jnp.broadcast_to(value[None], (lax.axis_size(axis),) + value.shape)
    return lax.all_to_all(spread, axis, 0, 0)


def body(tokens, cotangent, pad_mask, rewards, selected, gate_weight, up_weight, down_weight):
    n_y = lax.axis_size("y")
    n_k = lax.axis_size("zhi")
    y = lax.axis_index("y")
    rows, width = tokens.shape
    units = gate_weight.shape[1]
    block = lax.axis_index(ROW) * n_k + lax.axis_index("zhi")
    copies = lax.axis_size(("zlo", "x"))
    half = copies * rows
    part = half // n_y
    share = 2 * part
    quarter = width // n_k

    spread = prepare(copies, block, rewards, selected, pad_mask, tokens, cotangent)
    mine = lax.all_to_all(spread, ("zlo", "x"), 0, 0)
    other = shift(mine, "core", 1).reshape(half, 2 * width)
    mine = mine.reshape(half, 2 * width)
    own_cuts = lax.all_to_all(cut_quarters(n_k, mine), "zhi", 0, 0)

    pieces = []
    for rows_in in (mine, other):
        gate = jnp.dot(rows_in[:, :width], gate_weight, preferred_element_type=f32) * SCALE_UP
        up = jnp.dot(rows_in[:, :width], up_weight, preferred_element_type=f32) * SCALE_UP
        back = SCALE_BACK * lax.dot_general(
            rows_in[:, width:], down_weight, (((1,), (1,)), ((), ())), preferred_element_type=f32
        )
        whole = jnp.concatenate([gate, up, back], axis=1).astype(f16)
        pieces.append(whole.reshape(n_y, part, 3 * units))
    partial_sums = after(jnp.concatenate(pieces, axis=1), own_cuts)
    sums = jnp.sum(lax.all_to_all(partial_sums, "y", 0, 0).astype(f32), axis=0)

    gate_value = sums[:, :units] * (1.0 / SCALE_UP)
    up_value = sums[:, units : 2 * units] * (1.0 / SCALE_UP)
    back_value = sums[:, 2 * units :] * (1.0 / SCALE_BACK)
    sigmoid_gate = jax.nn.sigmoid(gate_value)
    active = gate_value * sigmoid_gate
    hidden = (active * up_value).astype(bf16)
    gate_back = (
        back_value * up_value * sigmoid_gate * (1.0 + gate_value * (1.0 - sigmoid_gate))
    ).astype(bf16)
    up_back = (back_value * active).astype(bf16)
    values = jnp.concatenate([hidden, gate_back, up_back], axis=1)
    near = copies_to(values, "zhi").reshape(n_k * share, 3 * units)

    order = [0]
    for s in range(1, n_y // 2):
        order += [s, n_y - s]
    order.append(n_y // 2)
    other_cuts = shift(own_cuts, "core", 1)
    right = left = near
    held = {0: near}
    for s in range(1, n_y // 2):
        right = shift(right, "y", 1)
        left = shift(left, "y", -1)
        held[n_y - s] = right
        held[s] = left
        if s == 1:
            inputs = put_in_order(order, y, own_cuts, after(other_cuts, right, left))
    middle = near.shape[0] // 2
    top = shift(right[:middle], "y", 1)
    low = shift(left[middle:], "y", -1)
    return products(inputs, [held[r] for r in order[:-1]] + [top, low])


def solution(mesh):
    n_row, n_col, n_rep = mesh.devices.shape
    fine = Mesh(
        mesh.devices.reshape(Z_LO, n_row // (Z_LO * CORES), CORES, n_col, n_rep),
        ("zlo", "x", "core", "y", "zhi"),
    )
    blocks = ROW + ("zhi",)
    placed = (
        P(blocks, "y"),
        P(blocks, "y"),
        P(blocks),
        P(),
        P(),
        P("y", ROW),
        P("y", ROW),
        P(ROW, "y"),
    )
    return jax.shard_map(
        body,
        mesh=fine,
        in_specs=placed,
        out_specs=(P(("y", "zhi"), ROW), P(("y", "zhi"), ROW), P(ROW, ("y", "zhi"))),
        check_vma=False,
    )
```

```python
import functools

import jax
import jax.numpy as jnp
from jax import lax
from jax.experimental import pallas as pl
from jax.experimental.pallas import tpu as pltpu
from jax.sharding import Mesh
from jax.sharding import PartitionSpec as P

SAMPLES = 8
COMP_LEN = 16
CORES = 2
Z_LO = 2
SCALE_UP = 128.0
SCALE_BACK = 1024.0
ROW = ("zlo", "x", "core")
bf16 = jnp.bfloat16
f16 = jnp.float16
f32 = jnp.float32


def shift(value, axis, step):
    n = lax.axis_size(axis)
    return lax.ppermute(value, axis, [(i, (i + step) % n) for i in range(n)])


def prepare_kernel(block_ref, rewards_ref, selected_ref, pad_ref, tokens_ref, cotangent_ref, all_ref):
    rows, width = tokens_ref.shape
    completion = block_ref[0] * rows // COMP_LEN
    prompt = completion // SAMPLES
    sample = completion % SAMPLES
    reward = rewards_ref[prompt, sample].astype(f32)
    chosen = jnp.where(selected_ref[prompt] == sample, 1.0, 0.0)
    factor = reward / 4.0 + chosen
    row = lax.broadcasted_iota(jnp.int32, (rows, 1), 0)
    weight = jnp.zeros((rows, 1), f32)
    for n in range(rows):
        weight = jnp.where(row == n, pad_ref[n].astype(f32) * factor, weight)
    grads = (weight * cotangent_ref[...].astype(f32)).astype(bf16)
    for copy in range(all_ref.shape[0]):
        all_ref[copy, :, :width] = tokens_ref[...]
        all_ref[copy, :, width:] = grads


def in_vmem():
    return pl.BlockSpec(memory_space=pltpu.VMEM)


def in_smem():
    return pl.BlockSpec(memory_space=pltpu.SMEM)


def limit(mebibytes):
    return pltpu.CompilerParams(vmem_limit_bytes=mebibytes * 1024 * 1024)


def prepare(copies, block, rewards, selected, pad_mask, tokens, cotangent):
    rows, width = tokens.shape
    return pl.pallas_call(
        prepare_kernel,
        out_shape=jax.ShapeDtypeStruct((copies, rows, 2 * width), bf16),
        in_specs=[in_smem()] * 4 + [in_vmem()] * 2,
        out_specs=in_vmem(),
    )(block.reshape(1), rewards, selected, pad_mask, tokens, cotangent)


def cut_kernel(rows_ref, out_ref):
    n_k = out_ref.shape[0]
    width = rows_ref.shape[1] // 2
    quarter = width // n_k
    for t in range(n_k):
        out_ref[t, :, :quarter] = rows_ref[:, t * quarter : (t + 1) * quarter]
        out_ref[t, :, quarter:] = rows_ref[:, width + t * quarter : width + (t + 1) * quarter]


def cut_quarters(n_k, rows):
    return pl.pallas_call(
        cut_kernel,
        out_shape=jax.ShapeDtypeStruct((n_k, rows.shape[0], rows.shape[1] // n_k), bf16),
        in_specs=[in_vmem()],
        out_specs=in_vmem(),
        compiler_params=limit(4),
    )(rows)


def order_kernel(order, y_ref, own_ref, other_ref, *out_refs):
    n_k, rows, _ = own_ref.shape
    n_y = len(order)
    part = rows // n_y
    for r, out_ref in zip(order, out_refs):
        share = lax.rem(y_ref[0] + r, n_y)
        spot = pl.ds(pl.multiple_of(share * part, part), part)
        at = 0
        for t in range(n_k):
            for ref in (own_ref, other_ref):
                out_ref[at : at + part, :] = ref[t, spot, :]
                at += part


def put_in_order(order, y, own, other):
    n_k, rows, both = own.shape
    n_y = len(order)
    out = jax.ShapeDtypeStruct((2 * n_k * rows // n_y, both), bf16)
    pieces = pl.pallas_call(
        functools.partial(order_kernel, order),
        out_shape=(out,) * n_y,
        in_specs=[in_smem(), in_vmem(), in_vmem()],
        out_specs=(in_vmem(),) * n_y,
        compiler_params=limit(8),
    )(y.reshape(1), own, other)
    return dict(zip(order, pieces))


def product(a, b):
    return lax.dot_general(a, b, (((0,), (0,)), ((), ())), preferred_element_type=f32)


def add_kernel(blocks, *refs):
    down_ref, gate_ref, up_ref = refs[-3:]
    earlier = refs[2 * blocks : -3]
    quarter, units = gate_ref.shape
    sums = [ref[...] for ref in earlier]
    for n in range(blocks):
        inputs_ref = refs[n]
        values_ref = refs[blocks + n]
        tokens = inputs_ref[:, :quarter]
        terms = (
            product(values_ref[:, :units], inputs_ref[:, quarter:]),
            product(tokens, values_ref[:, units : 2 * units]),
            product(tokens, values_ref[:, 2 * units :]),
        )
        sums = [a + b for a, b in zip(sums, terms)] if sums else terms
    down_ref[...], gate_ref[...], up_ref[...] = sums


def add_products(sums, inputs, values):
    blocks = len(values)
    quarter = inputs[0].shape[1] // 2
    rows, width = values[0].shape
    units = width // 3
    wide = jax.ShapeDtypeStruct((quarter, units), f32)
    tall = jax.ShapeDtypeStruct((units, quarter), f32)
    operands = tuple(inputs) + tuple(values) + tuple(sums)
    first = 2 * blocks
    return pl.pallas_call(
        functools.partial(add_kernel, blocks),
        out_shape=(tall, wide, wide),
        in_specs=[in_vmem()] * len(operands),
        out_specs=(in_vmem(),) * 3,
        input_output_aliases={first + n: n for n in range(len(sums))},
        compiler_params=limit(12),
        cost_estimate=pl.CostEstimate(
            flops=6 * blocks * rows * quarter * units,
            bytes_accessed=2 * blocks * rows * width,
            transcendentals=0,
        ),
    )(*operands)


def after(value, *others):
    return lax.optimization_barrier((value,) + others)[0]


def copies_to(value, axis):
    spread = jnp.broadcast_to(value[None], (lax.axis_size(axis),) + value.shape)
    return lax.all_to_all(spread, axis, 0, 0)


def body(tokens, cotangent, pad_mask, rewards, selected, gate_weight, up_weight, down_weight):
    n_y = lax.axis_size("y")
    n_k = lax.axis_size("zhi")
    y = lax.axis_index("y")
    rows, width = tokens.shape
    units = gate_weight.shape[1]
    block = lax.axis_index(ROW) * n_k + lax.axis_index("zhi")
    copies = lax.axis_size(("zlo", "x"))
    half = copies * rows
    part = half // n_y
    share = 2 * part
    quarter = width // n_k

    spread = prepare(copies, block, rewards, selected, pad_mask, tokens, cotangent)
    mine = lax.all_to_all(spread, ("zlo", "x"), 0, 0)
    other = shift(mine, "core", 1).reshape(half, 2 * width)
    mine = mine.reshape(half, 2 * width)
    own_cuts = lax.all_to_all(cut_quarters(n_k, mine), "zhi", 0, 0)

    pieces = []
    for rows_in in (mine, other):
        gate = jnp.dot(rows_in[:, :width], gate_weight, preferred_element_type=f32) * SCALE_UP
        up = jnp.dot(rows_in[:, :width], up_weight, preferred_element_type=f32) * SCALE_UP
        back = SCALE_BACK * lax.dot_general(
            rows_in[:, width:], down_weight, (((1,), (1,)), ((), ())), preferred_element_type=f32
        )
        whole = jnp.concatenate([gate, up, back], axis=1).astype(f16)
        pieces.append(whole.reshape(n_y, part, 3 * units))
    partial_sums = after(jnp.concatenate(pieces, axis=1), own_cuts)
    sums = jnp.sum(lax.all_to_all(partial_sums, "y", 0, 0).astype(f32), axis=0)

    gate_value = sums[:, :units] * (1.0 / SCALE_UP)
    up_value = sums[:, units : 2 * units] * (1.0 / SCALE_UP)
    back_value = sums[:, 2 * units :] * (1.0 / SCALE_BACK)
    sigmoid_gate = jax.nn.sigmoid(gate_value)
    active = gate_value * sigmoid_gate
    hidden = (active * up_value).astype(bf16)
    gate_back = (
        back_value * up_value * sigmoid_gate * (1.0 + gate_value * (1.0 - sigmoid_gate))
    ).astype(bf16)
    up_back = (back_value * active).astype(bf16)
    values = jnp.concatenate([hidden, gate_back, up_back], axis=1)
    near = copies_to(values, "zhi").reshape(n_k * share, 3 * units)

    order = [0]
    for s in range(1, n_y // 2):
        order += [s, n_y - s]
    order.append(n_y // 2)
    inputs = put_in_order(order, y, own_cuts, shift(own_cuts, "core", 1))
    right = left = near
    sums = ()
    for s in range(1, n_y // 2):
        right = shift(right, "y", 1)
        left = shift(left, "y", -1)
        rows_in = [inputs[n_y - s], inputs[s]]
        blocks = [right, left]
        if s == 1:
            rows_in.append(inputs[0])
            blocks.append(near)
        sums = add_products(sums, rows_in, blocks)
    middle = near.shape[0] // 2
    top = shift(right[:middle], "y", 1)
    low = shift(left[middle:], "y", -1)
    at = inputs[n_y // 2]
    down_grad, gate_grad, up_grad = add_products(sums, [at[:middle], at[middle:]], [top, low])
    return (gate_grad, up_grad, down_grad)


def solution(mesh):
    n_row, n_col, n_rep = mesh.devices.shape
    fine = Mesh(
        mesh.devices.reshape(Z_LO, n_row // (Z_LO * CORES), CORES, n_col, n_rep),
        ("zlo", "x", "core", "y", "zhi"),
    )
    blocks = ROW + ("zhi",)
    placed = (
        P(blocks, "y"),
        P(blocks, "y"),
        P(blocks),
        P(),
        P(),
        P("y", ROW),
        P("y", ROW),
        P(ROW, "y"),
    )
    return jax.shard_map(
        body,
        mesh=fine,
        in_specs=placed,
        out_specs=(P(("y", "zhi"), ROW), P(("y", "zhi"), ROW), P(ROW, ("y", "zhi"))),
        check_vma=False,
    )
```

```python
import functools

import jax
import jax.numpy as jnp
from jax import lax
from jax.experimental import pallas as pl
from jax.experimental.pallas import tpu as pltpu
from jax.sharding import Mesh
from jax.sharding import PartitionSpec as P

SAMPLES = 8
COMP_LEN = 16
CORES = 2
Z_LO = 2
SCALE_UP = 128.0
SCALE_BACK = 1024.0
ROW = ("zlo", "x", "core")
bf16 = jnp.bfloat16
f16 = jnp.float16
f32 = jnp.float32


def shift(value, axis, step):
    n = lax.axis_size(axis)
    return lax.ppermute(value, axis, [(i, (i + step) % n) for i in range(n)])


def prepare_kernel(block_ref, rewards_ref, selected_ref, pad_ref, tokens_ref, cotangent_ref, all_ref):
    rows, width = tokens_ref.shape
    completion = block_ref[0] * rows // COMP_LEN
    prompt = completion // SAMPLES
    sample = completion % SAMPLES
    reward = rewards_ref[prompt, sample].astype(f32)
    chosen = jnp.where(selected_ref[prompt] == sample, 1.0, 0.0)
    factor = reward / 4.0 + chosen
    row = lax.broadcasted_iota(jnp.int32, (rows, 1), 0)
    weight = jnp.zeros((rows, 1), f32)
    for n in range(rows):
        weight = jnp.where(row == n, pad_ref[n].astype(f32) * factor, weight)
    grads = (weight * cotangent_ref[...].astype(f32)).astype(bf16)
    for copy in range(all_ref.shape[0]):
        all_ref[copy, :, :width] = tokens_ref[...]
        all_ref[copy, :, width:] = grads


def in_vmem():
    return pl.BlockSpec(memory_space=pltpu.VMEM)


def in_smem():
    return pl.BlockSpec(memory_space=pltpu.SMEM)


def limit(mebibytes):
    return pltpu.CompilerParams(vmem_limit_bytes=mebibytes * 1024 * 1024)


def prepare(copies, block, rewards, selected, pad_mask, tokens, cotangent):
    rows, width = tokens.shape
    return pl.pallas_call(
        prepare_kernel,
        out_shape=jax.ShapeDtypeStruct((copies, rows, 2 * width), bf16),
        in_specs=[in_smem()] * 4 + [in_vmem()] * 2,
        out_specs=in_vmem(),
    )(block.reshape(1), rewards, selected, pad_mask, tokens, cotangent)


def cut_kernel(rows_ref, out_ref):
    n_k = out_ref.shape[0]
    width = rows_ref.shape[1] // 2
    quarter = width // n_k
    for t in range(n_k):
        out_ref[t, :, :quarter] = rows_ref[:, t * quarter : (t + 1) * quarter]
        out_ref[t, :, quarter:] = rows_ref[:, width + t * quarter : width + (t + 1) * quarter]


def cut_quarters(n_k, rows):
    return pl.pallas_call(
        cut_kernel,
        out_shape=jax.ShapeDtypeStruct((n_k, rows.shape[0], rows.shape[1] // n_k), bf16),
        in_specs=[in_vmem()],
        out_specs=in_vmem(),
        compiler_params=limit(4),
    )(rows)


def order_kernel(order, y_ref, own_ref, other_ref, *out_refs):
    n_k, rows, _ = own_ref.shape
    n_y = len(order)
    part = rows // n_y
    for r, out_ref in zip(order, out_refs):
        share = lax.rem(y_ref[0] + r, n_y)
        spot = pl.ds(pl.multiple_of(share * part, part), part)
        at = 0
        for t in range(n_k):
            for ref in (own_ref, other_ref):
                out_ref[at : at + part, :] = ref[t, spot, :]
                at += part


def put_in_order(order, y, own, other):
    n_k, rows, both = own.shape
    n_y = len(order)
    out = jax.ShapeDtypeStruct((2 * n_k * rows // n_y, both), bf16)
    pieces = pl.pallas_call(
        functools.partial(order_kernel, order),
        out_shape=(out,) * n_y,
        in_specs=[in_smem(), in_vmem(), in_vmem()],
        out_specs=(in_vmem(),) * n_y,
        compiler_params=limit(8),
    )(y.reshape(1), own, other)
    return dict(zip(order, pieces))


def product(a, b):
    return lax.dot_general(a, b, (((0,), (0,)), ((), ())), preferred_element_type=f32)


def add_products(sums, inputs, values):
    quarter = inputs.shape[1] // 2
    units = values.shape[1] // 3
    terms = (
        product(inputs[:, :quarter], values[:, units : 2 * units]),
        product(inputs[:, :quarter], values[:, 2 * units :]),
        product(values[:, :units], inputs[:, quarter:]),
    )
    return terms if sums is None else tuple(a + b for a, b in zip(sums, terms))


def after(value, *others):
    return lax.optimization_barrier((value,) + others)[0]


def copies_to(value, axis):
    spread = jnp.broadcast_to(value[None], (lax.axis_size(axis),) + value.shape)
    return lax.all_to_all(spread, axis, 0, 0)


def body(tokens, cotangent, pad_mask, rewards, selected, gate_weight, up_weight, down_weight):
    n_y = lax.axis_size("y")
    n_k = lax.axis_size("zhi")
    y = lax.axis_index("y")
    rows, width = tokens.shape
    units = gate_weight.shape[1]
    block = lax.axis_index(ROW) * n_k + lax.axis_index("zhi")
    copies = lax.axis_size(("zlo", "x"))
    half = copies * rows
    part = half // n_y
    share = 2 * part
    quarter = width // n_k

    spread = prepare(copies, block, rewards, selected, pad_mask, tokens, cotangent)
    mine = lax.all_to_all(spread, ("zlo", "x"), 0, 0)
    other = shift(mine, "core", 1).reshape(half, 2 * width)
    mine = mine.reshape(half, 2 * width)
    own_cuts = lax.all_to_all(cut_quarters(n_k, mine), "zhi", 0, 0)

    pieces = []
    for rows_in in (mine, other):
        gate = jnp.dot(rows_in[:, :width], gate_weight, preferred_element_type=f32) * SCALE_UP
        up = jnp.dot(rows_in[:, :width], up_weight, preferred_element_type=f32) * SCALE_UP
        back = SCALE_BACK * lax.dot_general(
            rows_in[:, width:], down_weight, (((1,), (1,)), ((), ())), preferred_element_type=f32
        )
        whole = jnp.concatenate([gate, up, back], axis=1).astype(f16)
        pieces.append(whole.reshape(n_y, part, 3 * units))
    partial_sums = after(jnp.concatenate(pieces, axis=1), own_cuts)
    sums = jnp.sum(lax.all_to_all(partial_sums, "y", 0, 0).astype(f32), axis=0)

    gate_value = sums[:, :units] * (1.0 / SCALE_UP)
    up_value = sums[:, units : 2 * units] * (1.0 / SCALE_UP)
    back_value = sums[:, 2 * units :] * (1.0 / SCALE_BACK)
    sigmoid_gate = jax.nn.sigmoid(gate_value)
    active = gate_value * sigmoid_gate
    hidden = (active * up_value).astype(bf16)
    gate_back = (
        back_value * up_value * sigmoid_gate * (1.0 + gate_value * (1.0 - sigmoid_gate))
    ).astype(bf16)
    up_back = (back_value * active).astype(bf16)
    values = jnp.concatenate([hidden, gate_back, up_back], axis=1)
    near = copies_to(values, "zhi").reshape(n_k * share, 3 * units)

    order = [0]
    for s in range(1, n_y // 2):
        order += [s, n_y - s]
    order.append(n_y // 2)
    inputs = put_in_order(order, y, own_cuts, shift(own_cuts, "core", 1))
    right = left = near
    sums = None
    waiting = [(inputs[0], near)]
    for s in range(1, n_y // 2):
        right = shift(right, "y", 1)
        left = shift(left, "y", -1)
        rows_in, blocks = zip(*waiting)
        blocks = jnp.concatenate([after(v, right) for v in blocks], axis=0)
        sums = add_products(sums, jnp.concatenate(rows_in, axis=0), blocks)
        waiting = [(inputs[n_y - s], right), (inputs[s], left)]
    middle = near.shape[0] // 2
    top = shift(right[:middle], "y", 1)
    low = shift(left[middle:], "y", -1)
    for rows_in, block_in in waiting:
        sums = add_products(sums, rows_in, block_in)
    return add_products(sums, inputs[n_y // 2], jnp.concatenate([top, low], axis=0))


def solution(mesh):
    n_row, n_col, n_rep = mesh.devices.shape
    fine = Mesh(
        mesh.devices.reshape(Z_LO, n_row // (Z_LO * CORES), CORES, n_col, n_rep),
        ("zlo", "x", "core", "y", "zhi"),
    )
    blocks = ROW + ("zhi",)
    placed = (
        P(blocks, "y"),
        P(blocks, "y"),
        P(blocks),
        P(),
        P(),
        P("y", ROW),
        P("y", ROW),
        P(ROW, "y"),
    )
    return jax.shard_map(
        body,
        mesh=fine,
        in_specs=placed,
        out_specs=(P(("y", "zhi"), ROW), P(("y", "zhi"), ROW), P(ROW, ("y", "zhi"))),
        check_vma=False,
    )
```

```python
import functools

import jax
import jax.numpy as jnp
from jax import lax
from jax.experimental import pallas as pl
from jax.experimental.pallas import tpu as pltpu
from jax.sharding import Mesh
from jax.sharding import PartitionSpec as P

SAMPLES = 8
COMP_LEN = 16
CORES = 2
Z_LO = 2
SCALE_UP = 128.0
SCALE_BACK = 1024.0
ROW = ("zlo", "x", "core")
bf16 = jnp.bfloat16
f16 = jnp.float16
f32 = jnp.float32


def shift(value, axis, step):
    n = lax.axis_size(axis)
    return lax.ppermute(value, axis, [(i, (i + step) % n) for i in range(n)])


def ring_step(value):
    n = lax.axis_size("y")
    pairs = [(core * n + i, core * n + (i + 1 - 2 * core) % n) for core in range(CORES) for i in range(n)]
    return lax.ppermute(value, ("core", "y"), pairs)


def prepare_kernel(block_ref, rewards_ref, selected_ref, pad_ref, tokens_ref, cotangent_ref, all_ref):
    rows, width = tokens_ref.shape
    completion = block_ref[0] * rows // COMP_LEN
    prompt = completion // SAMPLES
    sample = completion % SAMPLES
    reward = rewards_ref[prompt, sample].astype(f32)
    chosen = jnp.where(selected_ref[prompt] == sample, 1.0, 0.0)
    factor = reward / 4.0 + chosen
    row = lax.broadcasted_iota(jnp.int32, (rows, 1), 0)
    weight = jnp.zeros((rows, 1), f32)
    for n in range(rows):
        weight = jnp.where(row == n, pad_ref[n].astype(f32) * factor, weight)
    grads = (weight * cotangent_ref[...].astype(f32)).astype(bf16)
    for copy in range(all_ref.shape[0]):
        all_ref[copy, :, :width] = tokens_ref[...]
        all_ref[copy, :, width:] = grads


def in_vmem():
    return pl.BlockSpec(memory_space=pltpu.VMEM)


def in_smem():
    return pl.BlockSpec(memory_space=pltpu.SMEM)


def limit(mebibytes):
    return pltpu.CompilerParams(vmem_limit_bytes=mebibytes * 1024 * 1024)


def prepare(copies, block, rewards, selected, pad_mask, tokens, cotangent):
    rows, width = tokens.shape
    return pl.pallas_call(
        prepare_kernel,
        out_shape=jax.ShapeDtypeStruct((copies, rows, 2 * width), bf16),
        in_specs=[in_smem()] * 4 + [in_vmem()] * 2,
        out_specs=in_vmem(),
    )(block.reshape(1), rewards, selected, pad_mask, tokens, cotangent)


def cut_kernel(rows_ref, out_ref):
    n_k = out_ref.shape[0]
    width = rows_ref.shape[1] // 2
    quarter = width // n_k
    for t in range(n_k):
        out_ref[t, :, :quarter] = rows_ref[:, t * quarter : (t + 1) * quarter]
        out_ref[t, :, quarter:] = rows_ref[:, width + t * quarter : width + (t + 1) * quarter]


def cut_quarters(n_k, rows):
    return pl.pallas_call(
        cut_kernel,
        out_shape=jax.ShapeDtypeStruct((n_k, rows.shape[0], rows.shape[1] // n_k), bf16),
        in_specs=[in_vmem()],
        out_specs=in_vmem(),
        compiler_params=limit(4),
    )(rows)


def order_kernel(place_ref, own_ref, other_ref, *out_refs):
    n_k, rows, _ = own_ref.shape
    n_y = len(out_refs)
    part = rows // n_y
    for s, out_ref in enumerate(out_refs):
        share = lax.rem(place_ref[0] + n_y + s * place_ref[1], n_y)
        spot = pl.ds(pl.multiple_of(share * part, part), part)
        at = 0
        for t in range(n_k):
            for ref in (own_ref, other_ref):
                out_ref[at : at + part, :] = ref[t, spot, :]
                at += part


def put_in_order(n_y, place, own, other):
    n_k, rows, both = own.shape
    out = jax.ShapeDtypeStruct((2 * n_k * rows // n_y, both), bf16)
    return pl.pallas_call(
        order_kernel,
        out_shape=(out,) * n_y,
        in_specs=[in_smem(), in_vmem(), in_vmem()],
        out_specs=(in_vmem(),) * n_y,
        compiler_params=limit(8),
    )(place, own, other)


def product(a, b):
    return lax.dot_general(a, b, (((0,), (0,)), ((), ())), preferred_element_type=f32)


def add_products(sums, inputs, values):
    quarter = inputs.shape[1] // 2
    units = values.shape[1] // 3
    terms = (
        product(inputs[:, :quarter], values[:, units : 2 * units]),
        product(inputs[:, :quarter], values[:, 2 * units :]),
        product(values[:, :units], inputs[:, quarter:]),
    )
    return terms if sums is None else tuple(a + b for a, b in zip(sums, terms))


def after(value, *others):
    return lax.optimization_barrier((value,) + others)[0]


def copies_to(value, axis):
    spread = jnp.broadcast_to(value[None], (lax.axis_size(axis),) + value.shape)
    return lax.all_to_all(spread, axis, 0, 0)


def body(tokens, cotangent, pad_mask, rewards, selected, gate_weight, up_weight, down_weight):
    n_y = lax.axis_size("y")
    n_k = lax.axis_size("zhi")
    rows, width = tokens.shape
    units = gate_weight.shape[1]
    block = lax.axis_index(ROW) * n_k + lax.axis_index("zhi")
    copies = lax.axis_size(("zlo", "x"))
    half = copies * rows
    part = half // n_y
    share = 2 * part
    quarter = width // n_k

    spread = prepare(copies, block, rewards, selected, pad_mask, tokens, cotangent)
    mine = lax.all_to_all(spread, ("zlo", "x"), 0, 0)
    other = shift(mine, "core", 1).reshape(half, 2 * width)
    mine = mine.reshape(half, 2 * width)
    own_cuts = lax.all_to_all(cut_quarters(n_k, mine), "zhi", 0, 0)

    pieces = []
    for rows_in in (mine, other):
        gate = jnp.dot(rows_in[:, :width], gate_weight, preferred_element_type=f32) * SCALE_UP
        up = jnp.dot(rows_in[:, :width], up_weight, preferred_element_type=f32) * SCALE_UP
        back = SCALE_BACK * lax.dot_general(
            rows_in[:, width:], down_weight, (((1,), (1,)), ((), ())), preferred_element_type=f32
        )
        whole = jnp.concatenate([gate, up, back], axis=1).astype(f16)
        pieces.append(whole.reshape(n_y, part, 3 * units))
    partial_sums = after(jnp.concatenate(pieces, axis=1), own_cuts)
    other_cuts = shift(own_cuts, "core", 1)
    sums = after(lax.all_to_all(partial_sums, "y", 0, 0), other_cuts)
    sums = jnp.sum(sums.astype(f32), axis=0)

    gate_value = sums[:, :units] * (1.0 / SCALE_UP)
    up_value = sums[:, units : 2 * units] * (1.0 / SCALE_UP)
    back_value = sums[:, 2 * units :] * (1.0 / SCALE_BACK)
    sigmoid_gate = jax.nn.sigmoid(gate_value)
    active = gate_value * sigmoid_gate
    hidden = (active * up_value).astype(bf16)
    gate_back = (
        back_value * up_value * sigmoid_gate * (1.0 + gate_value * (1.0 - sigmoid_gate))
    ).astype(bf16)
    up_back = (back_value * active).astype(bf16)
    values = jnp.concatenate([hidden, gate_back, up_back], axis=1)
    near = copies_to(values, "zhi").reshape(n_k * share, 3 * units)

    place = jnp.stack([lax.axis_index("y"), 2 * lax.axis_index("core") - 1])
    inputs = put_in_order(n_y, place, own_cuts, other_cuts)
    sums = None
    held = near
    for s in range(n_y - 1):
        arrived = ring_step(held)
        sums = lax.optimization_barrier(add_products(sums, inputs[s], held))
        held = arrived
    return add_products(sums, inputs[n_y - 1], held)


def solution(mesh):
    n_row, n_col, n_rep = mesh.devices.shape
    fine = Mesh(
        mesh.devices.reshape(Z_LO, n_row // (Z_LO * CORES), CORES, n_col, n_rep),
        ("zlo", "x", "core", "y", "zhi"),
    )
    blocks = ROW + ("zhi",)
    placed = (
        P(blocks, "y"),
        P(blocks, "y"),
        P(blocks),
        P(),
        P(),
        P("y", ROW),
        P("y", ROW),
        P(ROW, "y"),
    )
    return jax.shard_map(
        body,
        mesh=fine,
        in_specs=placed,
        out_specs=(P(("y", "zhi"), ROW), P(("y", "zhi"), ROW), P(ROW, ("y", "zhi"))),
        check_vma=False,
    )
```

```python
import functools

import jax
import jax.numpy as jnp
from jax import lax
from jax.experimental import pallas as pl
from jax.experimental.pallas import tpu as pltpu
from jax.sharding import Mesh
from jax.sharding import PartitionSpec as P

SAMPLES = 8
COMP_LEN = 16
CORES = 2
Z_LO = 2
SCALE_UP = 128.0
SCALE_BACK = 1024.0
ROW = ("zlo", "x", "core")
bf16 = jnp.bfloat16
f16 = jnp.float16
f32 = jnp.float32


def shift(value, axis, step):
    n = lax.axis_size(axis)
    return lax.ppermute(value, axis, [(i, (i + step) % n) for i in range(n)])


def prepare_kernel(block_ref, rewards_ref, selected_ref, pad_ref, tokens_ref, cotangent_ref, all_ref):
    rows, width = tokens_ref.shape
    completion = block_ref[0] * rows // COMP_LEN
    prompt = completion // SAMPLES
    sample = completion % SAMPLES
    reward = rewards_ref[prompt, sample].astype(f32)
    chosen = jnp.where(selected_ref[prompt] == sample, 1.0, 0.0)
    factor = reward / 4.0 + chosen
    row = lax.broadcasted_iota(jnp.int32, (rows, 1), 0)
    weight = jnp.zeros((rows, 1), f32)
    for n in range(rows):
        weight = jnp.where(row == n, pad_ref[n].astype(f32) * factor, weight)
    grads = (weight * cotangent_ref[...].astype(f32)).astype(bf16)
    for copy in range(all_ref.shape[0]):
        all_ref[copy, :, :width] = tokens_ref[...]
        all_ref[copy, :, width:] = grads


def in_vmem():
    return pl.BlockSpec(memory_space=pltpu.VMEM)


def in_smem():
    return pl.BlockSpec(memory_space=pltpu.SMEM)


def limit(mebibytes):
    return pltpu.CompilerParams(vmem_limit_bytes=mebibytes * 1024 * 1024)


def prepare(copies, block, rewards, selected, pad_mask, tokens, cotangent):
    rows, width = tokens.shape
    return pl.pallas_call(
        prepare_kernel,
        out_shape=jax.ShapeDtypeStruct((copies, rows, 2 * width), bf16),
        in_specs=[in_smem()] * 4 + [in_vmem()] * 2,
        out_specs=in_vmem(),
    )(block.reshape(1), rewards, selected, pad_mask, tokens, cotangent)


def cut_kernel(rows_ref, out_ref):
    n_k = out_ref.shape[0]
    width = rows_ref.shape[1] // 2
    quarter = width // n_k
    for t in range(n_k):
        out_ref[t, :, :quarter] = rows_ref[:, t * quarter : (t + 1) * quarter]
        out_ref[t, :, quarter:] = rows_ref[:, width + t * quarter : width + (t + 1) * quarter]


def cut_quarters(n_k, rows):
    return pl.pallas_call(
        cut_kernel,
        out_shape=jax.ShapeDtypeStruct((n_k, rows.shape[0], rows.shape[1] // n_k), bf16),
        in_specs=[in_vmem()],
        out_specs=in_vmem(),
        compiler_params=limit(4),
    )(rows)


def order_kernel(order, y_ref, own_ref, other_ref, out_ref):
    n_k, rows, _ = own_ref.shape
    n_y = len(order)
    part = rows // n_y
    at = 0
    for r in order:
        share = lax.rem(y_ref[0] + r, n_y)
        spot = pl.ds(pl.multiple_of(share * part, part), part)
        for t in range(n_k):
            for ref in (own_ref, other_ref):
                out_ref[at : at + part, :] = ref[t, spot, :]
                at += part


def put_in_order(order, y, own, other):
    n_k, rows, both = own.shape
    return pl.pallas_call(
        functools.partial(order_kernel, order),
        out_shape=jax.ShapeDtypeStruct((2 * n_k * rows, both), bf16),
        in_specs=[in_smem(), in_vmem(), in_vmem()],
        out_specs=in_vmem(),
        compiler_params=limit(8),
    )(y.reshape(1), own, other)


def product(a, b):
    return lax.dot_general(a, b, (((0,), (0,)), ((), ())), preferred_element_type=f32)


def after(value, *others):
    return lax.optimization_barrier((value,) + others)[0]


def copies_to(value, axis):
    spread = jnp.broadcast_to(value[None], (lax.axis_size(axis),) + value.shape)
    return lax.all_to_all(spread, axis, 0, 0)


def body(tokens, cotangent, pad_mask, rewards, selected, gate_weight, up_weight, down_weight):
    n_y = lax.axis_size("y")
    n_k = lax.axis_size("zhi")
    y = lax.axis_index("y")
    rows, width = tokens.shape
    units = gate_weight.shape[1]
    block = lax.axis_index(ROW) * n_k + lax.axis_index("zhi")
    copies = lax.axis_size(("zlo", "x"))
    half = copies * rows
    part = half // n_y
    share = 2 * part
    quarter = width // n_k

    spread = prepare(copies, block, rewards, selected, pad_mask, tokens, cotangent)
    mine = lax.all_to_all(spread, ("zlo", "x"), 0, 0)
    other = shift(mine, "core", 1).reshape(half, 2 * width)
    mine = mine.reshape(half, 2 * width)
    own_cuts = lax.all_to_all(cut_quarters(n_k, mine), "zhi", 0, 0)

    pieces = []
    for rows_in in (mine, other):
        gate = jnp.dot(rows_in[:, :width], gate_weight, preferred_element_type=f32) * SCALE_UP
        up = jnp.dot(rows_in[:, :width], up_weight, preferred_element_type=f32) * SCALE_UP
        back = SCALE_BACK * lax.dot_general(
            rows_in[:, width:], down_weight, (((1,), (1,)), ((), ())), preferred_element_type=f32
        )
        whole = jnp.concatenate([gate, up, back], axis=1).astype(f16)
        pieces.append(whole.reshape(n_y, part, 3 * units))
    partial_sums = after(jnp.concatenate(pieces, axis=1), own_cuts)
    other_cuts = shift(own_cuts, "core", 1)
    sums = after(lax.all_to_all(partial_sums, "y", 0, 0), other_cuts)
    sums = jnp.sum(sums.astype(f32), axis=0)

    gate_value = sums[:, :units] * (1.0 / SCALE_UP)
    up_value = sums[:, units : 2 * units] * (1.0 / SCALE_UP)
    back_value = sums[:, 2 * units :] * (1.0 / SCALE_BACK)
    sigmoid_gate = jax.nn.sigmoid(gate_value)
    active = gate_value * sigmoid_gate
    hidden = (active * up_value).astype(bf16)
    gate_back = (
        back_value * up_value * sigmoid_gate * (1.0 + gate_value * (1.0 - sigmoid_gate))
    ).astype(bf16)
    up_back = (back_value * active).astype(bf16)
    values = jnp.concatenate([hidden, gate_back, up_back], axis=1)
    near = copies_to(values, "zhi").reshape(n_k * share, 3 * units)

    order = [0]
    for s in range(1, n_y // 2):
        order += [s, n_y - s]
    order.append(n_y // 2)
    inputs = put_in_order(order, y, own_cuts, other_cuts)
    right = left = near
    held = {0: near}
    for s in range(1, n_y // 2):
        right = shift(right, "y", 1)
        left = shift(left, "y", -1)
        held[n_y - s] = right
        held[s] = left
    middle = near.shape[0] // 2
    top = shift(right[:middle], "y", 1)
    low = shift(left[middle:], "y", -1)
    every = jnp.concatenate([held[r] for r in order[:-1]] + [top, low], axis=0)
    down_grad = product(every[:, :units], inputs[:, quarter:])
    gate_grad = product(inputs[:, :quarter], every[:, units : 2 * units])
    up_grad = product(inputs[:, :quarter], every[:, 2 * units :])
    return (gate_grad, up_grad, down_grad)


def solution(mesh):
    n_row, n_col, n_rep = mesh.devices.shape
    fine = Mesh(
        mesh.devices.reshape(Z_LO, n_row // (Z_LO * CORES), CORES, n_col, n_rep),
        ("zlo", "x", "core", "y", "zhi"),
    )
    blocks = ROW + ("zhi",)
    placed = (
        P(blocks, "y"),
        P(blocks, "y"),
        P(blocks),
        P(),
        P(),
        P("y", ROW),
        P("y", ROW),
        P(ROW, "y"),
    )
    return jax.shard_map(
        body,
        mesh=fine,
        in_specs=placed,
        out_specs=(P(("y", "zhi"), ROW), P(("y", "zhi"), ROW), P(ROW, ("y", "zhi"))),
        check_vma=False,
    )
```

```python
import functools

import jax
import jax.numpy as jnp
from jax import lax
from jax.experimental import pallas as pl
from jax.experimental.pallas import tpu as pltpu
from jax.sharding import Mesh
from jax.sharding import PartitionSpec as P

SAMPLES = 8
COMP_LEN = 16
CORES = 2
Z_LO = 2
SCALE_UP = 128.0
SCALE_BACK = 1024.0
ROW = ("zlo", "x", "core")
bf16 = jnp.bfloat16
f16 = jnp.float16
f32 = jnp.float32


def shift(value, axis, step):
    n = lax.axis_size(axis)
    return lax.ppermute(value, axis, [(i, (i + step) % n) for i in range(n)])


def prepare_kernel(block_ref, rewards_ref, selected_ref, pad_ref, tokens_ref, cotangent_ref, all_ref):
    rows, width = tokens_ref.shape
    completion = block_ref[0] * rows // COMP_LEN
    prompt = completion // SAMPLES
    sample = completion % SAMPLES
    reward = rewards_ref[prompt, sample].astype(f32)
    chosen = jnp.where(selected_ref[prompt] == sample, 1.0, 0.0)
    factor = reward / 4.0 + chosen
    row = lax.broadcasted_iota(jnp.int32, (rows, 1), 0)
    weight = jnp.zeros((rows, 1), f32)
    for n in range(rows):
        weight = jnp.where(row == n, pad_ref[n].astype(f32) * factor, weight)
    grads = (weight * cotangent_ref[...].astype(f32)).astype(bf16)
    for copy in range(all_ref.shape[0]):
        all_ref[copy, :, :width] = tokens_ref[...]
        all_ref[copy, :, width:] = grads


def in_vmem():
    return pl.BlockSpec(memory_space=pltpu.VMEM)


def in_smem():
    return pl.BlockSpec(memory_space=pltpu.SMEM)


def limit(mebibytes):
    return pltpu.CompilerParams(vmem_limit_bytes=mebibytes * 1024 * 1024)


def prepare(copies, block, rewards, selected, pad_mask, tokens, cotangent):
    rows, width = tokens.shape
    return pl.pallas_call(
        prepare_kernel,
        out_shape=jax.ShapeDtypeStruct((copies, rows, 2 * width), bf16),
        in_specs=[in_smem()] * 4 + [in_vmem()] * 2,
        out_specs=in_vmem(),
    )(block.reshape(1), rewards, selected, pad_mask, tokens, cotangent)


def cut_kernel(k_ref, rows_ref, *out_refs):
    n_k = len(out_refs)
    width = rows_ref.shape[1] // 2
    quarter = width // n_k
    for t, out_ref in enumerate(out_refs):
        owner = lax.rem(k_ref[0] + n_k - t, n_k)
        at = pl.multiple_of(owner * quarter, quarter)
        out_ref[:, :quarter] = rows_ref[:, pl.ds(at, quarter)]
        out_ref[:, quarter:] = rows_ref[:, pl.ds(width + at, quarter)]


def cut_quarters(n_k, k, rows):
    out = jax.ShapeDtypeStruct((rows.shape[0], rows.shape[1] // n_k), bf16)
    return pl.pallas_call(
        cut_kernel,
        out_shape=(out,) * n_k,
        in_specs=[in_smem(), in_vmem()],
        out_specs=(in_vmem(),) * n_k,
        compiler_params=limit(4),
    )(k.reshape(1), rows)


def order_kernel(order, place_ref, own_ref, other_ref, out_ref):
    n_k, rows, _ = own_ref.shape
    n_y = len(order)
    part = rows // n_y
    at = 0
    for r in order:
        share = lax.rem(place_ref[0] + r, n_y)
        spot = pl.ds(pl.multiple_of(share * part, part), part)
        for t in range(n_k):
            source = lax.rem(t + n_k - place_ref[1], n_k)
            for ref in (own_ref, other_ref):
                out_ref[at : at + part, :] = ref[source, spot, :]
                at += part


def put_in_order(order, place, own, other):
    n_k, rows, both = own.shape
    return pl.pallas_call(
        functools.partial(order_kernel, order),
        out_shape=jax.ShapeDtypeStruct((2 * n_k * rows, both), bf16),
        in_specs=[in_smem(), in_vmem(), in_vmem()],
        out_specs=in_vmem(),
        compiler_params=limit(8),
    )(place, own, other)


def product(a, b):
    return lax.dot_general(a, b, (((0,), (0,)), ((), ())), preferred_element_type=f32)


def after(value, *others):
    return lax.optimization_barrier((value,) + others)[0]


def copies_to(value, axis):
    spread = jnp.broadcast_to(value[None], (lax.axis_size(axis),) + value.shape)
    return lax.all_to_all(spread, axis, 0, 0)


def body(tokens, cotangent, pad_mask, rewards, selected, gate_weight, up_weight, down_weight):
    n_y = lax.axis_size("y")
    n_k = lax.axis_size("zhi")
    y = lax.axis_index("y")
    rows, width = tokens.shape
    units = gate_weight.shape[1]
    k = lax.axis_index("zhi")
    block = lax.axis_index(ROW) * n_k + k
    copies = lax.axis_size(("zlo", "x"))
    half = copies * rows
    part = half // n_y
    share = 2 * part
    quarter = width // n_k

    spread = prepare(copies, block, rewards, selected, pad_mask, tokens, cotangent)
    mine = lax.all_to_all(spread, ("zlo", "x"), 0, 0)
    other = shift(mine, "core", 1).reshape(half, 2 * width)
    mine = mine.reshape(half, 2 * width)

    pieces = []
    for rows_in in (mine, other):
        gate = jnp.dot(rows_in[:, :width], gate_weight, preferred_element_type=f32) * SCALE_UP
        up = jnp.dot(rows_in[:, :width], up_weight, preferred_element_type=f32) * SCALE_UP
        back = SCALE_BACK * lax.dot_general(
            rows_in[:, width:], down_weight, (((1,), (1,)), ((), ())), preferred_element_type=f32
        )
        whole = jnp.concatenate([gate, up, back], axis=1).astype(f16)
        pieces.append(whole.reshape(n_y, part, 3 * units))
    partial_sums = jnp.concatenate(pieces, axis=1)
    cuts = cut_quarters(n_k, k, mine)
    cuts = lax.optimization_barrier(tuple(cuts) + (partial_sums,))[:n_k]
    own_cuts = [cuts[0]] + [shift(cuts[t], "zhi", -t) for t in range(1, n_k)]
    sums = after(lax.all_to_all(partial_sums, "y", 0, 0), *own_cuts)
    own_cuts = jnp.stack(own_cuts, axis=0)
    other_cuts = shift(own_cuts, "core", 1)
    sums = jnp.sum(sums.astype(f32), axis=0)

    gate_value = sums[:, :units] * (1.0 / SCALE_UP)
    up_value = sums[:, units : 2 * units] * (1.0 / SCALE_UP)
    back_value = sums[:, 2 * units :] * (1.0 / SCALE_BACK)
    sigmoid_gate = jax.nn.sigmoid(gate_value)
    active = gate_value * sigmoid_gate
    hidden = (active * up_value).astype(bf16)
    gate_back = (
        back_value * up_value * sigmoid_gate * (1.0 + gate_value * (1.0 - sigmoid_gate))
    ).astype(bf16)
    up_back = (back_value * active).astype(bf16)
    values = jnp.concatenate([hidden, gate_back, up_back], axis=1)
    near = after(copies_to(values, "zhi"), other_cuts).reshape(n_k * share, 3 * units)

    order = [0]
    for s in range(1, n_y // 2):
        order += [s, n_y - s]
    order.append(n_y // 2)
    inputs = put_in_order(order, jnp.stack([y, k]), own_cuts, other_cuts)
    right = left = near
    held = {0: near}
    for s in range(1, n_y // 2):
        right = shift(right, "y", 1)
        left = shift(left, "y", -1)
        held[n_y - s] = right
        held[s] = left
    middle = near.shape[0] // 2
    top = shift(right[:middle], "y", 1)
    low = shift(left[middle:], "y", -1)
    every = jnp.concatenate([held[r] for r in order[:-1]] + [top, low], axis=0)
    down_grad = product(every[:, :units], inputs[:, quarter:])
    gate_grad = product(inputs[:, :quarter], every[:, units : 2 * units])
    up_grad = product(inputs[:, :quarter], every[:, 2 * units :])
    return (gate_grad, up_grad, down_grad)


def solution(mesh):
    n_row, n_col, n_rep = mesh.devices.shape
    fine = Mesh(
        mesh.devices.reshape(Z_LO, n_row // (Z_LO * CORES), CORES, n_col, n_rep),
        ("zlo", "x", "core", "y", "zhi"),
    )
    blocks = ROW + ("zhi",)
    placed = (
        P(blocks, "y"),
        P(blocks, "y"),
        P(blocks),
        P(),
        P(),
        P("y", ROW),
        P("y", ROW),
        P(ROW, "y"),
    )
    return jax.shard_map(
        body,
        mesh=fine,
        in_specs=placed,
        out_specs=(P(("y", "zhi"), ROW), P(("y", "zhi"), ROW), P(ROW, ("y", "zhi"))),
        check_vma=False,
    )
```

```python
import functools

import jax
import jax.numpy as jnp
from jax import lax
from jax.experimental import pallas as pl
from jax.experimental.pallas import tpu as pltpu
from jax.sharding import Mesh
from jax.sharding import PartitionSpec as P

SAMPLES = 8
COMP_LEN = 16
CORES = 2
Z_LO = 2
SCALE_UP = 128.0
SCALE_BACK = 1024.0
ROW = ("zlo", "x", "core")
bf16 = jnp.bfloat16
f16 = jnp.float16
f32 = jnp.float32


def shift(value, axis, step):
    n = lax.axis_size(axis)
    return lax.ppermute(value, axis, [(i, (i + step) % n) for i in range(n)])


def prepare_kernel(block_ref, rewards_ref, selected_ref, pad_ref, tokens_ref, cotangent_ref, all_ref):
    rows, width = tokens_ref.shape
    completion = block_ref[0] * rows // COMP_LEN
    prompt = completion // SAMPLES
    sample = completion % SAMPLES
    reward = rewards_ref[prompt, sample].astype(f32)
    chosen = jnp.where(selected_ref[prompt] == sample, 1.0, 0.0)
    factor = reward / 4.0 + chosen
    row = lax.broadcasted_iota(jnp.int32, (rows, 1), 0)
    weight = jnp.zeros((rows, 1), f32)
    for n in range(rows):
        weight = jnp.where(row == n, pad_ref[n].astype(f32) * factor, weight)
    grads = (weight * cotangent_ref[...].astype(f32)).astype(bf16)
    for copy in range(all_ref.shape[0]):
        all_ref[copy, :, :width] = tokens_ref[...]
        all_ref[copy, :, width:] = grads


def in_vmem():
    return pl.BlockSpec(memory_space=pltpu.VMEM)


def in_smem():
    return pl.BlockSpec(memory_space=pltpu.SMEM)


def limit(mebibytes):
    return pltpu.CompilerParams(vmem_limit_bytes=mebibytes * 1024 * 1024)


def prepare(copies, block, rewards, selected, pad_mask, tokens, cotangent):
    rows, width = tokens.shape
    return pl.pallas_call(
        prepare_kernel,
        out_shape=jax.ShapeDtypeStruct((copies, rows, 2 * width), bf16),
        in_specs=[in_smem()] * 4 + [in_vmem()] * 2,
        out_specs=in_vmem(),
    )(block.reshape(1), rewards, selected, pad_mask, tokens, cotangent)


def cut_kernel(k_ref, rows_ref, *out_refs):
    n_k = len(out_refs)
    width = rows_ref.shape[1] // 2
    quarter = width // n_k
    for t, out_ref in enumerate(out_refs):
        owner = lax.rem(k_ref[0] + n_k - t, n_k)
        at = pl.multiple_of(owner * quarter, quarter)
        out_ref[:, :quarter] = rows_ref[:, pl.ds(at, quarter)]
        out_ref[:, quarter:] = rows_ref[:, pl.ds(width + at, quarter)]


def cut_quarters(n_k, k, rows):
    out = jax.ShapeDtypeStruct((rows.shape[0], rows.shape[1] // n_k), bf16)
    return pl.pallas_call(
        cut_kernel,
        out_shape=(out,) * n_k,
        in_specs=[in_smem(), in_vmem()],
        out_specs=(in_vmem(),) * n_k,
        compiler_params=limit(4),
    )(k.reshape(1), rows)


def order_kernel(order, place_ref, own_ref, other_ref, out_ref):
    n_k, rows, _ = own_ref.shape
    n_y = len(order)
    part = rows // n_y
    at = 0
    for r in order:
        share = lax.rem(place_ref[0] + r, n_y)
        spot = pl.ds(pl.multiple_of(share * part, part), part)
        for t in range(n_k):
            for ref in (own_ref, other_ref):
                out_ref[at : at + part, :] = ref[t, spot, :]
                at += part


def put_in_order(order, place, own, other):
    n_k, rows, both = own.shape
    return pl.pallas_call(
        functools.partial(order_kernel, order),
        out_shape=jax.ShapeDtypeStruct((2 * n_k * rows, both), bf16),
        in_specs=[in_smem(), in_vmem(), in_vmem()],
        out_specs=in_vmem(),
        compiler_params=limit(8),
    )(place, own, other)


def product(a, b):
    return lax.dot_general(a, b, (((0,), (0,)), ((), ())), preferred_element_type=f32)


def after(value, *others):
    return lax.optimization_barrier((value,) + others)[0]


def copies_to(value, axis):
    spread = jnp.broadcast_to(value[None], (lax.axis_size(axis),) + value.shape)
    return lax.all_to_all(spread, axis, 0, 0)


def body(tokens, cotangent, pad_mask, rewards, selected, gate_weight, up_weight, down_weight):
    n_y = lax.axis_size("y")
    n_k = lax.axis_size("zhi")
    y = lax.axis_index("y")
    rows, width = tokens.shape
    units = gate_weight.shape[1]
    k = lax.axis_index("zhi")
    block = lax.axis_index(ROW) * n_k + k
    copies = lax.axis_size(("zlo", "x"))
    half = copies * rows
    part = half // n_y
    share = 2 * part
    quarter = width // n_k

    spread = prepare(copies, block, rewards, selected, pad_mask, tokens, cotangent)
    mine = lax.all_to_all(spread, ("zlo", "x"), 0, 0)
    other = shift(mine, "core", 1).reshape(half, 2 * width)
    mine = mine.reshape(half, 2 * width)

    pieces = []
    for rows_in in (mine, other):
        gate = jnp.dot(rows_in[:, :width], gate_weight, preferred_element_type=f32) * SCALE_UP
        up = jnp.dot(rows_in[:, :width], up_weight, preferred_element_type=f32) * SCALE_UP
        back = SCALE_BACK * lax.dot_general(
            rows_in[:, width:], down_weight, (((1,), (1,)), ((), ())), preferred_element_type=f32
        )
        whole = jnp.concatenate([gate, up, back], axis=1).astype(f16)
        pieces.append(whole.reshape(n_y, part, 3 * units))
    partial_sums = jnp.concatenate(pieces, axis=1)
    cuts = cut_quarters(n_k, k, mine)
    cuts = lax.optimization_barrier(tuple(cuts) + (partial_sums,))[:n_k]
    own_cuts = [cuts[0]] + [shift(cuts[t], "zhi", -t) for t in range(1, n_k)]
    sums = after(lax.all_to_all(partial_sums, "y", 0, 0), *own_cuts)
    own_cuts = jnp.stack(own_cuts, axis=0)
    other_cuts = shift(own_cuts, "core", 1)
    sums = jnp.sum(sums.astype(f32), axis=0)

    gate_value = sums[:, :units] * (1.0 / SCALE_UP)
    up_value = sums[:, units : 2 * units] * (1.0 / SCALE_UP)
    back_value = sums[:, 2 * units :] * (1.0 / SCALE_BACK)
    sigmoid_gate = jax.nn.sigmoid(gate_value)
    active = gate_value * sigmoid_gate
    hidden = (active * up_value).astype(bf16)
    gate_back = (
        back_value * up_value * sigmoid_gate * (1.0 + gate_value * (1.0 - sigmoid_gate))
    ).astype(bf16)
    up_back = (back_value * active).astype(bf16)
    values = jnp.concatenate([hidden, gate_back, up_back], axis=1)
    replicas = after(copies_to(values, "zhi"), other_cuts)
    turned = jnp.concatenate([replicas, replicas[:-1]], axis=0)
    near = lax.dynamic_slice_in_dim(turned, k + 1, n_k - 1, axis=0)
    near = near.reshape((n_k - 1) * share, 3 * units)

    order = [0]
    for s in range(1, n_y // 2):
        order += [s, n_y - s]
    order.append(n_y // 2)
    inputs = put_in_order(order, y.reshape(1), own_cuts, other_cuts)
    rest = near.shape[0]
    right_1 = shift(values, "y", 1)
    left_1 = shift(values, "y", -1)
    right_2 = shift(right_1, "y", 1)
    left_2 = shift(left_1, "y", -1)
    own = {0: values, n_y - 1: right_1, 1: left_1, n_y - 2: right_2, 2: left_2}
    right = shift(jnp.concatenate([near, right_2], axis=0), "y", 1)
    left = shift(jnp.concatenate([near, left_2[part:], left_2[:part]], axis=0), "y", -1)
    own = {r: after(block, right) for r, block in own.items()}
    own[n_y - 3] = right[rest:]
    own[3] = jnp.concatenate([left[rest + part :], left[rest : rest + part]], axis=0)
    far = {0: near, n_y - 1: right[:rest], 1: left[:rest]}
    right = shift(right[: rest + part], "y", 1)
    left = shift(left[: rest + part], "y", -1)
    own[n_y // 2] = jnp.concatenate([right[rest:], left[rest:]], axis=0)
    far[n_y - 2] = right[:rest]
    far[2] = left[:rest]
    right = shift(right[:rest], "y", 1)
    left = shift(left[:rest], "y", -1)
    far[n_y - 3] = right
    far[3] = left
    middle = rest // 2
    top = shift(right[:middle], "y", 1)
    low = shift(left[middle:], "y", -1)
    blocks = [block for r in order[:-1] for block in (own[r], far[r])]
    every = jnp.concatenate(blocks + [own[n_y // 2], top, low], axis=0)
    down_grad = product(every[:, :units], inputs[:, quarter:])
    gate_grad = product(inputs[:, :quarter], every[:, units : 2 * units])
    up_grad = product(inputs[:, :quarter], every[:, 2 * units :])
    return (gate_grad, up_grad, down_grad)


def solution(mesh):
    n_row, n_col, n_rep = mesh.devices.shape
    fine = Mesh(
        mesh.devices.reshape(Z_LO, n_row // (Z_LO * CORES), CORES, n_col, n_rep),
        ("zlo", "x", "core", "y", "zhi"),
    )
    blocks = ROW + ("zhi",)
    placed = (
        P(blocks, "y"),
        P(blocks, "y"),
        P(blocks),
        P(),
        P(),
        P("y", ROW),
        P("y", ROW),
        P(ROW, "y"),
    )
    return jax.shard_map(
        body,
        mesh=fine,
        in_specs=placed,
        out_specs=(P(("y", "zhi"), ROW), P(("y", "zhi"), ROW), P(ROW, ("y", "zhi"))),
        check_vma=False,
    )
```

```python
import functools

import jax
import jax.numpy as jnp
from jax import lax
from jax.experimental import pallas as pl
from jax.experimental.pallas import tpu as pltpu
from jax.sharding import Mesh
from jax.sharding import PartitionSpec as P

SAMPLES = 8
COMP_LEN = 16
CORES = 2
Z_LO = 2
SCALE_UP = 128.0
SCALE_BACK = 1024.0
ROW = ("zlo", "x", "core")
bf16 = jnp.bfloat16
f16 = jnp.float16
f32 = jnp.float32


def shift(value, axis, step):
    n = lax.axis_size(axis)
    return lax.ppermute(value, axis, [(i, (i + step) % n) for i in range(n)])


def prepare_kernel(block_ref, rewards_ref, selected_ref, pad_ref, tokens_ref, cotangent_ref, all_ref):
    rows, width = tokens_ref.shape
    completion = block_ref[0] * rows // COMP_LEN
    prompt = completion // SAMPLES
    sample = completion % SAMPLES
    reward = rewards_ref[prompt, sample].astype(f32)
    chosen = jnp.where(selected_ref[prompt] == sample, 1.0, 0.0)
    factor = reward / 4.0 + chosen
    row = lax.broadcasted_iota(jnp.int32, (rows, 1), 0)
    weight = jnp.zeros((rows, 1), f32)
    for n in range(rows):
        weight = jnp.where(row == n, pad_ref[n].astype(f32) * factor, weight)
    grads = (weight * cotangent_ref[...].astype(f32)).astype(bf16)
    for copy in range(all_ref.shape[0]):
        all_ref[copy, :, :width] = tokens_ref[...]
        all_ref[copy, :, width:] = grads


def in_vmem():
    return pl.BlockSpec(memory_space=pltpu.VMEM)


def in_smem():
    return pl.BlockSpec(memory_space=pltpu.SMEM)


def limit(mebibytes):
    return pltpu.CompilerParams(vmem_limit_bytes=mebibytes * 1024 * 1024)


def prepare(copies, block, rewards, selected, pad_mask, tokens, cotangent):
    rows, width = tokens.shape
    return pl.pallas_call(
        prepare_kernel,
        out_shape=jax.ShapeDtypeStruct((copies, rows, 2 * width), bf16),
        in_specs=[in_smem()] * 4 + [in_vmem()] * 2,
        out_specs=in_vmem(),
    )(block.reshape(1), rewards, selected, pad_mask, tokens, cotangent)


def cut_kernel(k_ref, rows_ref, *out_refs):
    n_k = len(out_refs)
    width = rows_ref.shape[1] // 2
    quarter = width // n_k
    for t, out_ref in enumerate(out_refs):
        owner = lax.rem(k_ref[0] + n_k - t, n_k)
        at = pl.multiple_of(owner * quarter, quarter)
        out_ref[:, :quarter] = rows_ref[:, pl.ds(at, quarter)]
        out_ref[:, quarter:] = rows_ref[:, pl.ds(width + at, quarter)]


def cut_quarters(n_k, k, rows):
    out = jax.ShapeDtypeStruct((rows.shape[0], rows.shape[1] // n_k), bf16)
    return pl.pallas_call(
        cut_kernel,
        out_shape=(out,) * n_k,
        in_specs=[in_smem(), in_vmem()],
        out_specs=(in_vmem(),) * n_k,
        compiler_params=limit(4),
    )(k.reshape(1), rows)


def order_kernel(order, place_ref, own_ref, other_ref, out_ref):
    n_k, rows, _ = own_ref.shape
    n_y = len(order)
    part = rows // n_y
    at = 0
    for r in order:
        share = lax.rem(place_ref[0] + r, n_y)
        spot = pl.ds(pl.multiple_of(share * part, part), part)
        for t in range(n_k):
            source = lax.rem(t + n_k - place_ref[1], n_k)
            for ref in (own_ref, other_ref):
                out_ref[at : at + part, :] = ref[source, spot, :]
                at += part


def put_in_order(order, place, own, other):
    n_k, rows, both = own.shape
    return pl.pallas_call(
        functools.partial(order_kernel, order),
        out_shape=jax.ShapeDtypeStruct((2 * n_k * rows, both), bf16),
        in_specs=[in_smem(), in_vmem(), in_vmem()],
        out_specs=in_vmem(),
        compiler_params=limit(8),
    )(place, own, other)


def product(a, b):
    return lax.dot_general(a, b, (((0,), (0,)), ((), ())), preferred_element_type=f32)


def after(value, *others):
    return lax.optimization_barrier((value,) + others)[0]


def body(tokens, cotangent, pad_mask, rewards, selected, gate_weight, up_weight, down_weight):
    n_y = lax.axis_size("y")
    n_k = lax.axis_size("zhi")
    y = lax.axis_index("y")
    rows, width = tokens.shape
    units = gate_weight.shape[1]
    k = lax.axis_index("zhi")
    block = lax.axis_index(ROW) * n_k + k
    copies = lax.axis_size(("zlo", "x"))
    half = copies * rows
    part = half // n_y
    share = 2 * part
    quarter = width // n_k

    spread = prepare(copies, block, rewards, selected, pad_mask, tokens, cotangent)
    mine = lax.all_to_all(spread, ("zlo", "x"), 0, 0)
    other = shift(mine, "core", 1).reshape(half, 2 * width)
    mine = mine.reshape(half, 2 * width)

    pieces = []
    for rows_in in (mine, other):
        gate = jnp.dot(rows_in[:, :width], gate_weight, preferred_element_type=f32) * SCALE_UP
        up = jnp.dot(rows_in[:, :width], up_weight, preferred_element_type=f32) * SCALE_UP
        back = SCALE_BACK * lax.dot_general(
            rows_in[:, width:], down_weight, (((1,), (1,)), ((), ())), preferred_element_type=f32
        )
        whole = jnp.concatenate([gate, up, back], axis=1).astype(f16)
        pieces.append(whole.reshape(n_y, part, 3 * units))
    partial_sums = jnp.concatenate(pieces, axis=1)
    cuts = cut_quarters(n_k, k, mine)
    cuts = lax.optimization_barrier(tuple(cuts) + (partial_sums,))[:n_k]
    own_cuts = [cuts[0]] + [shift(cuts[t], "zhi", -t) for t in range(1, n_k)]
    sums = after(lax.all_to_all(partial_sums, "y", 0, 0), *own_cuts)
    own_cuts = jnp.stack(own_cuts, axis=0)
    other_cuts = shift(own_cuts, "core", 1)
    sums = jnp.sum(sums.astype(f32), axis=0)

    gate_value = sums[:, :units] * (1.0 / SCALE_UP)
    up_value = sums[:, units : 2 * units] * (1.0 / SCALE_UP)
    back_value = sums[:, 2 * units :] * (1.0 / SCALE_BACK)
    sigmoid_gate = jax.nn.sigmoid(gate_value)
    active = gate_value * sigmoid_gate
    hidden = (active * up_value).astype(bf16)
    gate_back = (
        back_value * up_value * sigmoid_gate * (1.0 + gate_value * (1.0 - sigmoid_gate))
    ).astype(bf16)
    up_back = (back_value * active).astype(bf16)
    values = jnp.concatenate([hidden, gate_back, up_back], axis=1)
    near = after(lax.all_gather(values, "zhi"), other_cuts).reshape(n_k * share, 3 * units)

    order = [0]
    for s in range(1, n_y // 2):
        order += [s, n_y - s]
    order.append(n_y // 2)
    inputs = put_in_order(order, jnp.stack([y, k]), own_cuts, other_cuts)
    right = left = near
    held = {0: near}
    for s in range(1, n_y // 2):
        right = shift(right, "y", 1)
        left = shift(left, "y", -1)
        held[n_y - s] = right
        held[s] = left
    middle = near.shape[0] // 2
    top = shift(right[:middle], "y", 1)
    low = shift(left[middle:], "y", -1)
    every = jnp.concatenate([held[r] for r in order[:-1]] + [top, low], axis=0)
    down_grad = product(every[:, :units], inputs[:, quarter:])
    gate_grad = product(inputs[:, :quarter], every[:, units : 2 * units])
    up_grad = product(inputs[:, :quarter], every[:, 2 * units :])
    return (gate_grad, up_grad, down_grad)


def solution(mesh):
    n_row, n_col, n_rep = mesh.devices.shape
    fine = Mesh(
        mesh.devices.reshape(Z_LO, n_row // (Z_LO * CORES), CORES, n_col, n_rep),
        ("zlo", "x", "core", "y", "zhi"),
    )
    blocks = ROW + ("zhi",)
    placed = (
        P(blocks, "y"),
        P(blocks, "y"),
        P(blocks),
        P(),
        P(),
        P("y", ROW),
        P("y", ROW),
        P(ROW, "y"),
    )
    return jax.shard_map(
        body,
        mesh=fine,
        in_specs=placed,
        out_specs=(P(("y", "zhi"), ROW), P(("y", "zhi"), ROW), P(ROW, ("y", "zhi"))),
        check_vma=False,
    )
```
